32 devices in a mesh: leaf: 8 (over z, x), row: 4 (over y, core).
Axes of the slice: x: 2, y: 2, z: 4, core: 2. Of those that a mesh axis runs over, the one named last changes fastest.
Arguments:
- right_side: float32 [8, 2048, 1024], P('leaf', 'row'), may hold values from -6 to 6
- lower_rows: float32 [8, 2048, 2048], P('leaf', 'row'), may hold values from -0.125 to 0.125
- diag_inverse: float32 [8, 2048, 512], P('leaf', 'row'), may hold values from -0.25 to 0.25
- update_rows: float32 [8, 4096, 2048], P('leaf', 'row'), may hold values from -0.125 to 0.125
- owner_map: int32 [8, 32], P('leaf', 'row'), may hold values from 0 to 63, as said below
- block_counts: int32 [8], P('leaf'), may hold values from 1 to 32, as said below
- ancestor_rhs: float32 [8, 4096, 1024], P('leaf', 'row'), may hold values from -6 to 6
- ancestor_inverse: float32 [8, 4096, 128], P('leaf', 'row'), may hold values from -0.5 to 0.5
Outputs:
- solution: float32 [8, 2048, 1024], P('leaf', 'row')
- parent_front_solution_rows: float32 [8, 4096, 1024], P('leaf', 'row')
The draws below stay inside these ranges and needn't reach their ends.
Inputs may be any that keep to these rules, and one draw needn't show every extreme that they name: `owner_map`: among the 8 blocks b with the same b // 8 of one front, the values g // 8 are distinct. `block_counts`: some front has all its blocks live.
All inputs are finite; a program needn't handle non-finite values.
Results may differ from the reference program's by a relative error of at most 0.0001.
Values sent between devices are 32-bit elements; how exact they have to be, the bound alone decides.
No kernel may reach another device: no remote copies, remote signals or barrier semaphores. Data moves between devices by JAX's collectives and lax.ppermute only.
A program may use at most 320 MiB of HBM per device.

```python
import jax
import jax.numpy as jnp
from jax import lax

PIV = 2048
UPD = 4096
BLK = 128
RHS = 1024
TB = 8
FRONTS = 8
PANEL = 512
N_ROW = 4


def draw_owner_map(key, part):
    nblocks = UPD // N_ROW // BLK
    keys = jax.random.split(key, 2)
    total = FRONTS * N_ROW
    owner_keys = jax.random.split(keys[0], total)
    owners = jax.vmap(lambda k: jax.random.permutation(k, FRONTS)[:nblocks])(owner_keys)
    slots = jax.random.randint(keys[1], (total, nblocks), 0, TB)
    return (owners * TB + slots).reshape(FRONTS, N_ROW * nblocks).astype(jnp.int32)


def draw_block_counts(key, part):
    whole = UPD // BLK
    keys = jax.random.split(key, 2)
    counts = jax.random.randint(keys[0], (FRONTS,), 1, whole + 1)
    pick = jax.random.randint(keys[1], (), 0, FRONTS)
    return jnp.where(jnp.arange(FRONTS) == pick, whole, counts).astype(jnp.int32)


def levels(stream_key, dims, pieces, least, high):
    factor_of, own = 1.0, jax.random.fold_in(stream_key, 6)
    for dim, parts in pieces:
        steps = jnp.exp(jax.random.uniform(jax.random.fold_in(own, dim), (parts,), jnp.float32, least / len(pieces), high / len(pieces)))
        factor_of = factor_of * jnp.repeat(steps, dims[dim] // parts).reshape([-1 if axis == dim else 1 for axis in range(len(dims))])
    return factor_of


def noise(own_key, extent, spread, most, cuts=(), kind=jnp.bfloat16):
    values = spread * jax.random.normal(own_key, extent, jnp.float32)
    if cuts:
        values = values * levels(own_key, extent, cuts, -0.22, 0.18)
    return jnp.clip(values, -most, most).astype(kind)


def setup_inputs(seed: int = 0) -> dict:
    streams_of = jax.random.split(jax.random.key(seed), 9)
    right_side = noise(streams_of[0], (FRONTS, PIV, RHS), 1.0, 6.0, ((0, 8), (1, 4)), jnp.float32)
    lower_rows = noise(streams_of[1], (FRONTS, PIV, PIV), PIV ** -0.5, 0.125, ((0, 8), (1, 4)), jnp.float32)
    diag_inverse = noise(streams_of[2], (FRONTS, PIV, PANEL), PANEL ** -0.5, 0.25, ((0, 8), (1, 4)), jnp.float32)
    update_rows = noise(streams_of[3], (FRONTS, UPD, PIV), PIV ** -0.5, 0.125, ((0, 8), (1, 4)), jnp.float32)
    owner_map = draw_owner_map(jax.random.fold_in(streams_of[8], 71), 0)
    block_counts = draw_block_counts(jax.random.fold_in(streams_of[8], 71), 0)
    ancestor_rhs = noise(streams_of[6], (FRONTS, N_ROW * TB * BLK, RHS), 1.0, 6.0, ((0, 8), (1, 4)), jnp.float32)
    ancestor_inverse = noise(streams_of[7], (FRONTS, N_ROW * TB * BLK, BLK), BLK ** -0.5, 0.5, ((0, 8), (1, 4)), jnp.float32)
    return {"right_side": right_side, "lower_rows": lower_rows, "diag_inverse": diag_inverse, "update_rows": update_rows, "owner_map": owner_map, "block_counts": block_counts, "ancestor_rhs": ancestor_rhs, "ancestor_inverse": ancestor_inverse}


def reference(right_side, lower_rows, diag_inverse, update_rows, owner_map, block_counts, ancestor_rhs, ancestor_inverse):
    topmost_front = lax.Precision.HIGHEST
    panel = PIV // N_ROW
    nblocks = UPD // N_ROW // BLK
    solved = []
    for k in range(N_ROW):
        accum = jnp.zeros((FRONTS, panel, RHS), jnp.float32)
        for j in range(k):
            block = lower_rows[:, k * panel:(k + 1) * panel, j * panel:(j + 1) * panel]
            accum = accum + jnp.einsum("fpq,fqc->fpc", block, solved[j], precision=topmost_front)
        inverse = diag_inverse[:, k * panel:(k + 1) * panel, :]
        solved.append(jnp.einsum("fpq,fqc->fpc", inverse, right_side[:, k * panel:(k + 1) * panel] - accum, precision=topmost_front))
    solution = jnp.concatenate(solved, axis=1)
    update = jnp.einsum("fuq,fqc->fuc", update_rows, solution, precision=topmost_front)
    blocks = update.reshape(FRONTS, N_ROW, nblocks, BLK, RHS)
    index = jnp.arange(N_ROW * nblocks, dtype=jnp.int32).reshape(N_ROW, nblocks)
    live = (index[None] < block_counts[:, None, None]).astype(jnp.float32)
    targets = owner_map.reshape(FRONTS, N_ROW, nblocks)
    onehot = (targets[..., None] == jnp.arange(FRONTS * TB, dtype=jnp.int32)).astype(jnp.float32) * live[..., None]
    summed = jnp.einsum("frjg,frjbc->rgbc", onehot, blocks, precision=topmost_front)
    summed = summed.reshape(N_ROW, FRONTS, TB, BLK, RHS).transpose(1, 0, 2, 3, 4).reshape(FRONTS, N_ROW * TB, BLK, RHS)
    remaining_right_side = ancestor_rhs.reshape(FRONTS, N_ROW * TB, BLK, RHS) - summed
    inverse = ancestor_inverse.reshape(FRONTS, N_ROW * TB, BLK, BLK)
    parent_front_solution_rows = jnp.einsum("fnab,fnbc->fnac", inverse, remaining_right_side, precision=topmost_front)
    return solution, parent_front_solution_rows.reshape(FRONTS, N_ROW * TB * BLK, RHS)
```

```python
import functools

import jax
import jax.numpy as jnp
from jax import lax
from jax.experimental import pallas as pl
from jax.experimental.pallas import tpu as pltpu
from jax.sharding import PartitionSpec as P

BLK = 128
PAIR = 2
TILE = 128
TAIL = 8
LAG = 2
VMEM_LIMIT = 16 * 1024 * 1024
FIRST_LIMIT = 56 * 1024 * 1024
F32 = jnp.float32
BF16 = jnp.bfloat16
ANY = pl.BlockSpec(memory_space=pl.ANY)
HBM = pl.BlockSpec(memory_space=pltpu.HBM)
VMEM = pl.BlockSpec(memory_space=pltpu.VMEM)
SMEM = pl.BlockSpec(memory_space=pltpu.SMEM)


def widths_of(half):
    assert half % TILE == 0
    return [TILE // 2] * 2 + [TILE] * (half // TILE - 1)


def mxu(a, b):
    return jnp.dot(a, b, preferred_element_type=F32)


def split(x):
    high = x.astype(BF16)
    return high, (x - high.astype(F32)).astype(BF16)


def both_terms(x):
    return jnp.concatenate(split(x), axis=1)


def product(high, low, x):
    w = x.shape[1] // 2
    wide = mxu(high, x)
    return wide[:, :w] + (wide[:, w:] + mxu(low, x[:, :w]))


def times(a, b):
    return product(*split(a), both_terms(b))


def f32(*shape):
    return jax.ShapeDtypeStruct(shape, F32)


def bf16(*shape):
    return jax.ShapeDtypeStruct(shape, BF16)


def packed(rows, w):
    return (rows, TILE) if w < TILE else (PAIR * rows, w)


def put(ref, at, even, odd):
    rows, w = even.shape
    if w < TILE:
        ref[at : at + rows, :] = jnp.concatenate([even, odd], axis=1)
    else:
        ref[at : at + rows, :] = even
        ref[at + rows : at + PAIR * rows, :] = odd


def get(ref, at, rows, w):
    if w < TILE:
        both = ref[at : at + rows, :]
        return both[:, :w], both[:, w:]
    return ref[at : at + rows, :], ref[at + rows : at + PAIR * rows, :]


def call(kernel, in_specs, out_specs, out_shape, operands, after=(), scratch=(), aliases=None, limit=VMEM_LIMIT):
    n = len(operands)
    extra = len(after)

    def run(*refs):
        kernel(*refs[:n], *refs[n + extra :])

    return pl.pallas_call(
        run,
        in_specs=list(in_specs) + [ANY] * extra,
        out_specs=out_specs,
        out_shape=out_shape,
        scratch_shapes=scratch,
        input_output_aliases=aliases or {},
        compiler_params=pltpu.CompilerParams(vmem_limit_bytes=limit),
        cost_estimate=pl.CostEstimate(flops=1, bytes_accessed=1, transcendentals=0),
    )(*operands, *after)


def fetch(pairs, sems):
    copies = [pltpu.make_async_copy(a, b, sems.at[i]) for i, (a, b) in enumerate(pairs)]
    for copy in copies:
        copy.start()
    return copies


def factor_kernel(inv, inv_sib, col, col_sib, even_h, even_l, odd_h, odd_l, cross_h, cross_l):
    def fill(even, odd, cross):
        even_h[...], even_l[...] = split(even[...])
        odd_h[...], odd_l[...] = split(odd[...])
        cross_h[...], cross_l[...] = split(cross[...])

    @pl.when(lax.axis_index("row") % PAIR == 1)
    def _():
        fill(inv_sib, inv, col)

    @pl.when(lax.axis_index("row") % PAIR == 0)
    def _():
        fill(inv, inv_sib, col_sib)


def left_kernel(left, left_sib, high, low):
    panel = left.shape[0]

    def fill(even, odd):
        high[:panel, :], low[:panel, :] = split(even[...])
        high[panel:, :], low[panel:, :] = split(odd[...])

    @pl.when(lax.axis_index("row") % PAIR == 1)
    def _():
        fill(left_sib, left)

    @pl.when(lax.axis_index("row") % PAIR == 0)
    def _():
        fill(left, left_sib)


def cut_kernel(cuts, n, *refs):
    srcs, outs, sems = refs[:n], refs[n:-1], refs[-1]
    odd = lax.rem(lax.axis_index("row"), PAIR)
    pairs = []
    for (k, kind), out in zip(cuts, outs):
        w = out.shape[1]
        at = {"first": 0, "mine": odd * w, "other": (1 - odd) * w, "panel": (lax.axis_index("row") // PAIR) * PAIR * w}[kind]
        for r in range(0, out.shape[0], TILE):
            rows = pl.ds(r, TILE)
            pairs.append((srcs[k].at[rows, pl.ds(pl.multiple_of(at, TILE), w)], out.at[rows, :]))
    for copy in fetch(pairs, sems):
        copy.wait()


def block_at(place, row, n_leaf, targets_per, nblocks, leaf, owners, counts):
    dest = leaf ^ place
    source, has, slot = jnp.int32(0), jnp.int32(0), jnp.int32(-1)
    for b in range(nblocks):
        hit = (lax.div(owners[b], jnp.int32(targets_per)) == dest) & (row * nblocks + b < counts[0])
        source = jnp.where(hit, b, source)
        has = jnp.where(hit, 1, has)
        slot = jnp.where(hit, lax.rem(owners[b], jnp.int32(targets_per)), slot)
    return source, has, slot


def order_kernel(find, n_leaf, flip, owners, counts, rows, high, low, buf, sems):
    row = lax.axis_index("row") ^ flip
    found = [find(s, row, leaf=lax.axis_index("leaf"), owners=owners, counts=counts) for s in range(n_leaf)]

    def copy(s):
        at = pl.multiple_of(found[s][0] * BLK, BLK)
        return pltpu.make_async_copy(rows.at[pl.ds(at, BLK), :], buf.at[s % 4], sems.at[s % 4])

    ahead = min(3, n_leaf)
    for s in range(ahead):
        copy(s).start()
    for s in range(n_leaf):
        if s + ahead < n_leaf:
            copy(s + ahead).start()
        copy(s).wait()
        here = slice(s * BLK, (s + 1) * BLK)

        @pl.when(found[s][1] == 1)
        def _(here=here, s=s):
            high[here, :], low[here, :] = split(buf[s % 4])

        @pl.when(found[s][1] == 0)
        def _(here=here):
            high[here, :] = jnp.zeros((BLK, high.shape[1]), BF16)
            low[here, :] = jnp.zeros((BLK, high.shape[1]), BF16)


def lead_kernel(widths, *refs):
    (inv_e, inv_o, cross), refs = [refs[i : i + 2] for i in range(0, 6, 2)], refs[6:]
    rhs_own, rhs_sib, outs = refs[0], refs[1], refs[2:]
    w = sum(widths)
    odd = lax.axis_index("row") % PAIR == 1

    @pl.when(lax.axis_index("row") // PAIR == 0)
    def _():
        own, sib = rhs_own[:, :w], rhs_sib[:, :w]
        even, other = jnp.where(odd, sib, own), jnp.where(odd, own, sib)
        x_even = product(inv_e[0][...], inv_e[1][...], both_terms(even))
        other = other - product(cross[0][...], cross[1][...], both_terms(x_even))
        x_odd = product(inv_o[0][...], inv_o[1][...], both_terms(other))
        at = 0
        for part, out in zip(widths, outs):
            put(out, 0, x_even[:, at : at + part], x_odd[:, at : at + part])
            at += part


def step_kernel(tasks, n_out, *refs):
    (inv_e, inv_o, cross, left), refs = [refs[i : i + 2] for i in range(0, 8, 2)], refs[8:]
    rhs_own, rhs_sib, refs = refs[0], refs[1], refs[2:]
    outs = refs[-n_out:]
    odd = lax.axis_index("row") % PAIR == 1
    chip = lax.axis_index("row") // PAIR
    panel = rhs_own.shape[0]
    used = 0
    for stage, first, w, which in tasks:
        known = refs[used : used + stage]
        used += stage

        @pl.when(chip == stage)
        def _(stage=stage, first=first, w=w, known=known, out=outs[which]):
            own, sib = rhs_own[:, first : first + w], rhs_sib[:, first : first + w]
            even, other = jnp.where(odd, sib, own), jnp.where(odd, own, sib)
            if stage:
                x = jnp.concatenate([a for ref in known for a in get(ref, 0, panel, w)], axis=0)
                cols = slice(0, stage * PAIR * panel)
                gone = product(left[0][:, cols], left[1][:, cols], both_terms(x))
                even, other = even - gone[:panel], other - gone[panel:]
            x_even = product(inv_e[0][...], inv_e[1][...], both_terms(even))
            other = other - product(cross[0][...], cross[1][...], both_terms(x_even))
            x_odd = product(inv_o[0][...], inv_o[1][...], both_terms(other))
            put(out, 0, x_even, x_odd)


def update_kernel(n_chip, places, w, routes, tails, find, *refs):
    if tails is not None:
        owners, owners_sib, counts, refs = refs[0], refs[1], refs[2], refs[3:]
    high, low, high_sib, low_sib = refs[:4]
    n_in = 1 + max(routes.values())
    srcs, outs, x = refs[4 : 4 + n_in], refs[4 + n_in : -1], refs[-1]
    odd = lax.axis_index("row") % PAIR == 1
    chip = lax.axis_index("row") // PAIR
    panel = x.shape[0] // (PAIR * n_chip)
    for (y, j), k in routes.items():

        @pl.when(chip == y)
        def _(j=j, src=srcs[k]):
            even, other = get(src, 0, panel, w)
            at = j * PAIR * panel
            x[at : at + panel, :] = both_terms(even)
            x[at + panel : at + PAIR * panel, :] = both_terms(other)

    n_place = len(places)
    for s in sorted(range(0, n_place, PAIR), key=lambda s: -places[s][0]):
        rows = slice(s * BLK, (s + PAIR) * BLK)
        own = product(high[rows, :], low[rows, :], x[...])
        sib = product(high_sib[rows, :], low_sib[rows, :], x[...])
        even, other = jnp.where(odd, sib, own), jnp.where(odd, own, sib)
        for i in range(PAIR):
            k, at = places[s + i]
            part = slice(i * BLK, (i + 1) * BLK)
            put(outs[k], at, even[part], other[part])
    if tails is not None:
        for s, (k, at) in enumerate(tails):
            for flip, own_list in ((0, owners), (1, owners_sib)):
                row = lax.axis_index("row") ^ flip
                _, _, slot = find(s, row, leaf=lax.axis_index("leaf"), owners=own_list, counts=counts)
                here = pl.multiple_of(at + lax.rem(row, PAIR) * TAIL, TAIL)
                outs[k][pl.ds(here, TAIL), :] = jnp.full((TAIL, TILE), slot.astype(F32))


def sum_kernel(blocks, tail, w, n_src, merge, *refs):
    if tail is None:
        slots, refs = refs[0], refs[1:]
    srcs, refs = refs[:n_src], refs[n_src:]
    if merge:
        old_mine, old_theirs, refs = refs[0], refs[1], refs[2:]
    if tail is None:
        mine, theirs, total = refs
    else:
        mine, theirs, slots, total = refs
        for s, (k, at) in enumerate(blocks):
            for i in range(PAIR):
                here = slice(at + tail + i * TAIL, at + tail + (i + 1) * TAIL)
                slots[PAIR * s + i] = jnp.max(srcs[k][here, :]).astype(jnp.int32)
    odd = lax.axis_index("row") % PAIR == 1
    total[...] = jnp.zeros_like(total)
    for s, (k, at) in enumerate(blocks):
        got = get(srcs[k], at, BLK, w)
        for i in range(PAIR):
            slot = slots[PAIR * s + i]

            @pl.when(slot >= 0)
            def _(slot=slot, i=i, got=got):
                place = pl.ds(pl.multiple_of(slot * BLK, BLK), BLK)
                total[i, place, :] += got[i]

    a = jnp.where(odd, total[1], total[0])
    b = jnp.where(odd, total[0], total[1])
    if merge:
        a = jnp.concatenate([old_mine[...], a], axis=1)
        b = jnp.concatenate([old_theirs[...], b], axis=1)
    mine[...] = a
    theirs[...] = b


def solve_blocks(inv, rhs, at, total, put_rows):
    w = total.shape[1]
    for t in range(total.shape[0] // BLK):
        rows = slice(t * BLK, (t + 1) * BLK)
        put_rows(rows, times(inv[rows, :], rhs[rows, pl.ds(at, w)] - total[rows, :]))


def ancestor_kernel(half, cuts, inv, rhs, *refs):
    n = len(cuts)
    mine, other, outs = refs[:n], refs[n], refs[n + 1 :]
    odd = lax.rem(lax.axis_index("row"), PAIR)
    rows_all = inv.shape[0]
    for k, (first, _) in enumerate(cuts):
        for side, total, out in (
            (odd, mine[k], outs[k]),
            (1 - odd, other.at[k * rows_all : (k + 1) * rows_all, :], outs[n + k]),
        ):

            def put_rows(rows, x, out=out):
                out[rows, :] = x

            solve_blocks(inv, rhs, pl.multiple_of(side * half + first, TILE), total, put_rows)


def last_kernel(half, cuts, n_early, inv, rhs, panel_mine, panel_other, *refs):
    n = len(cuts)
    pieces, totals, out, solved = refs[: 2 * n_early], refs[2 * n_early : 2 * n], refs[2 * n], refs[2 * n + 1]
    scratch, sems = refs[2 * n + 2 : -1], refs[-1]
    odd = lax.rem(lax.axis_index("row"), PAIR)
    copies = []

    def send(src, dst, mine, first, w):
        at = pl.multiple_of((odd if mine else 1 - odd) * half + first, TILE)
        copy = pltpu.make_async_copy(src, dst.at[:, pl.ds(at, w)], sems.at[len(copies)])
        copy.start()
        copies.append(copy)

    for i in range(2 * n_early):
        send(pieces[i], out, i < n_early, *cuts[i % n_early])
    send(panel_mine, solved, True, 0, half)
    send(panel_other, solved, False, 0, half)
    late = n - n_early
    for i in range(2 * late):
        first, w = cuts[n_early + i % late]
        at = pl.multiple_of((odd if i < late else 1 - odd) * half + first, TILE)

        def put_rows(rows, x, buf=scratch[i]):
            buf[rows, :] = x

        solve_blocks(inv, rhs, at, totals[i], put_rows)
        send(scratch[i], out, i < late, first, w)
    for copy in copies:
        copy.wait()


def panels_kernel(chunks, n_chip, n_src, *refs):
    srcs, mine, theirs = refs[:n_src], refs[-2], refs[-1]
    odd = lax.axis_index("row") % PAIR == 1
    chip = lax.axis_index("row") // PAIR
    panel = mine.shape[0]
    for first, w, ks in chunks:
        for j in range(n_chip):

            @pl.when(chip == j)
            def _(src=srcs[ks[j]], first=first, w=w):
                even, other = get(src, 0, panel, w)
                mine[:, first : first + w] = jnp.where(odd, other, even)
                theirs[:, first : first + w] = jnp.where(odd, even, other)


def join_kernel(cuts, n, *refs):
    srcs, outs = refs[:n], refs[n:]
    for out, parts in zip(outs, cuts):
        at = 0
        for k, first, count in parts:
            out[at : at + count, :] = srcs[k][first : first + count, :]
            at += count


def body(
    right_side,
    lower_rows,
    diag_inverse,
    update_rows,
    owner_map,
    block_counts,
    ancestor_rhs,
    ancestor_inverse,
):
    n_row = lax.axis_size("row")
    n_leaf = lax.axis_size("leaf")
    my_row = lax.axis_index("row")
    my_leaf = lax.axis_index("leaf")
    side = my_row % PAIR
    n_chip = n_row // PAIR
    chip = my_row // PAIR
    rhs = right_side[0]
    lower = lower_rows[0]
    inverse = diag_inverse[0]
    update = update_rows[0]
    owners = owner_map[0]
    panel, columns = rhs.shape
    pair_rows = PAIR * panel
    half = columns // PAIR
    piv = update.shape[1]
    nblocks = update.shape[0] // BLK
    anc_rhs = ancestor_rhs[0]
    anc_inv = ancestor_inverse[0]
    anc_rows = anc_rhs.shape[0]
    targets_per = anc_rows // BLK

    widths = widths_of(half)
    offsets = [sum(widths[:i]) for i in range(len(widths))]
    n_chunk = len(widths)

    swap = [(r, r ^ 1) for r in range(n_row)]

    def sibling(a):
        return lax.ppermute(a, "row", swap)

    def across(a, mask):
        return lax.ppermute(a, "leaf", [(i, i ^ mask) for i in range(n_leaf)])

    def cut(arrays, cuts, after=(), limit=VMEM_LIMIT):
        return call(
            functools.partial(cut_kernel, [c[:2] for c in cuts], len(arrays)),
            [HBM] * len(arrays),
            [VMEM] * len(cuts),
            [f32(arrays[k].shape[0], w) for k, _, w in cuts],
            tuple(arrays),
            after=after,
            scratch=[pltpu.SemaphoreType.DMA((sum(arrays[k].shape[0] // TILE for k, _, _ in cuts),))],
            limit=limit,
        )

    col, rhs_own, rhs_out = cut([lower, rhs], [(0, "panel", panel), (1, "mine", half), (1, "other", half)], limit=FIRST_LIMIT)
    inv_sib = sibling(inverse)
    col_sib = sibling(col)
    rhs_sib = sibling(rhs_out)
    owners_sib = sibling(owners)
    before = max((n_chip - 1) * pair_rows, panel)

    factors = call(
        factor_kernel,
        [VMEM] * 4,
        [VMEM] * 6,
        [bf16(panel, panel)] * 6,
        (inverse, inv_sib, col, col_sib),
        after=(rhs_sib, owners_sib),
    )
    token = factors[0]
    left = None

    own = [[None] * n_chip for _ in range(n_chunk)]
    there = [[None] * n_chip for _ in range(n_chunk)]
    last_sent = []

    def step(tasks, after=()):
        nonlocal token, last_sent
        if not tasks:
            return
        kinds = sorted({widths[c] for _, c in tasks})
        known = [there[c][i][(j - i) % n_chip] for j, c in tasks for i in range(j)]
        lefts = left if left is not None else factors[4:6]
        outs = call(
            functools.partial(
                step_kernel, [(j, offsets[c], widths[c], kinds.index(widths[c])) for j, c in tasks], len(kinds)
            ),
            [VMEM] * (10 + len(known)),
            [VMEM] * len(kinds),
            [f32(*packed(panel, w)) for w in kinds],
            (*factors, *lefts, rhs_own, rhs_sib, *known),
            after=(token, *after),
        )
        token = outs[0]
        last_sent = []
        for w, out in zip(kinds, outs):
            here = [(j, c) for j, c in tasks if widths[c] == w]
            got = {}
            for k in range(1, n_chip):
                perm = []
                for j, _ in here:
                    to = (j + k) % n_chip
                    perm += [(PAIR * j + i, PAIR * to + i) for i in range(PAIR)]
                got[k] = lax.ppermute(out, "row", perm)
                last_sent.append(got[k])
            for j, c in here:
                own[c][j] = out
                there[c][j] = got

    def lead(n):
        nonlocal token
        outs = call(
            functools.partial(lead_kernel, widths[:n]),
            [VMEM] * 8,
            [VMEM] * n,
            [f32(*packed(panel, w)) for w in widths[:n]],
            (*factors, rhs_own, rhs_sib),
            after=(token,),
        )
        token = outs[0]
        for c, out in enumerate(outs):
            got = {}
            for k in range(1, n_chip):
                got[k] = lax.ppermute(out, "row", [(i, PAIR * k + i) for i in range(PAIR)])
            own[c][0] = out
            there[c][0] = got

    find = functools.partial(block_at, n_leaf=n_leaf, targets_per=targets_per, nblocks=nblocks)

    def order(rows, own_list, flip):
        nonlocal token
        outs = call(
            functools.partial(order_kernel, find, n_leaf, flip),
            [SMEM] * 2 + [HBM],
            [VMEM] * 2,
            [bf16(n_leaf * BLK, piv)] * 2,
            (own_list, block_counts, rows),
            after=(token,),
            scratch=[pltpu.VMEM((4, BLK, piv), F32), pltpu.SemaphoreType.DMA((4,))],
        )
        token = outs[0]
        return outs

    def join(arrays, cuts):
        nonlocal token
        outs = call(
            functools.partial(join_kernel, cuts, len(arrays)),
            [VMEM] * len(arrays),
            [VMEM] * len(cuts),
            [f32(sum(p[2] for p in parts), TILE) for parts in cuts],
            arrays,
            after=(token,),
        )
        token = outs[0]
        return outs

    far = sorted(range(2, n_leaf, 2), key=lambda m: (m & -m) * 2 * n_leaf - m, reverse=True)
    direct = [m + i for m in far for i in range(PAIR)] + [1]
    held, flown = {}, {}
    updates = ()

    def unit(c):
        return packed(BLK, widths[c])[0] + (PAIR * TAIL if c == 0 else 0)

    def fly(c, sends):
        flown.setdefault(c, [])
        for m, a, qs in sends:
            got = lax.ppermute(a, "leaf", [(i, i ^ m) for i in range(n_leaf)])
            flown[c].append(got)
            held[c] += [(got, i * unit(c), q ^ m, first) for i, (q, first) in enumerate(qs)]

    def push(c, after=()):
        nonlocal token
        w = widths[c]
        n = unit(c)
        if c + 1 < n_chunk:
            groups = [(0, [0, 1])] + [(m, [m, m + 1]) for m in far]
        else:
            groups = [(m, [m]) for m in [0] + direct]
        spots = {q: (k, i * n) for k, (_, qs) in enumerate(groups) for i, q in enumerate(qs)}
        places = [spots[q] for q in range(n_leaf)]
        tails = [(k, at + packed(BLK, w)[0]) for k, at in places] if c == 0 else None
        arrays, routes = [], {}
        for y in range(n_chip):
            for j in range(n_chip):
                a = own[c][j] if y == j else there[c][j][(y - j) % n_chip]
                k = next((k for k, b in enumerate(arrays) if b is a), len(arrays))
                if k == len(arrays):
                    arrays.append(a)
                routes[y, j] = k
        maps = (owners, owners_sib, block_counts) if c == 0 else ()
        outs = call(
            functools.partial(update_kernel, n_chip, places, w, routes, tails, find),
            [SMEM] * len(maps) + [VMEM] * (4 + len(arrays)),
            [VMEM] * len(groups),
            [f32(len(qs) * n, TILE) for _, qs in groups],
            (*maps, *updates, *arrays),
            after=(token, *after),
            scratch=[pltpu.VMEM((piv, 2 * w), BF16)],
        )
        token = outs[0]
        held[c] = [(outs[0], i * n, q, q) for i, q in enumerate(groups[0][1])]
        fly(c, [(m, a, [(q, q) for q in qs]) for (m, qs), a in zip(groups[1:], outs[1:])])

    def turn(c, after=()):
        nonlocal token
        n = unit(c)
        going = [b for b in held[c] if b[2] == 1]
        held[c] = [b for b in held[c] if b[2] == 0]
        arrays, parts = [], []
        for a, at, _, _ in going:
            k = next((k for k, b in enumerate(arrays) if b is a), len(arrays))
            if k == len(arrays):
                arrays.append(a)
            parts.append((k, at, n))
        (mixed,) = join(arrays, [parts], after)
        fly(c, [(1, mixed, [(q, first) for _, _, q, first in going])])

    def join(arrays, cuts, after=()):
        nonlocal token
        outs = call(
            functools.partial(join_kernel, cuts, len(arrays)),
            [VMEM] * len(arrays),
            [VMEM] * len(cuts),
            [f32(sum(p[2] for p in parts), TILE) for parts in cuts],
            arrays,
            after=(token, *after),
        )
        token = outs[0]
        return outs

    slots = None
    mine_cols, theirs_cols, cuts = [], [], []
    carry = None

    def finish(c, after=()):
        nonlocal token, slots, carry
        w = widths[c]
        arrays, blocks = [], []
        for a, at, _, _ in sorted(held[c], key=lambda b: b[3]):
            k = next((k for k, b in enumerate(arrays) if b is a), len(arrays))
            if k == len(arrays):
                arrays.append(a)
            blocks.append((k, at))
        tail = packed(BLK, w)[0] if c == 0 else None
        lookup = () if c == 0 else tuple(slots)
        merge = carry is not None
        hold = w < TILE and not merge
        shape = f32(anc_rows, 2 * w if merge else w)
        outs = call(
            functools.partial(sum_kernel, blocks, tail, w, len(arrays), merge),
            [SMEM] * len(lookup) + [VMEM] * (len(arrays) + (2 if merge else 0)),
            [VMEM] * 2 + ([SMEM] if c == 0 else []),
            [shape] * 2 + ([jax.ShapeDtypeStruct((n_leaf * PAIR,), jnp.int32)] if c == 0 else []),
            (*lookup, *arrays, *(carry or ())),
            after=(token, *after),
            scratch=[pltpu.VMEM((PAIR, anc_rows, w), F32)],
        )
        token = outs[0]
        if c == 0:
            slots = outs[2:]
        if hold:
            carry = (outs[0], outs[1])
            return
        carry = None
        mine_cols.append(outs[0])
        theirs_cols.append(outs[1])
        cuts.append((offsets[c] + w - shape.shape[1], shape.shape[1]))

    last = LAG * (n_chip - 1)
    left_own = lower[:, :before]
    left_sib = sibling(lax.optimization_barrier((left_own, token))[0])
    lead(2)
    update_sib = sibling(lax.optimization_barrier((update, token))[0])
    updates = tuple(order(update, owners, 0))
    left = call(
        left_kernel, [VMEM] * 2, [VMEM] * 2, [bf16(pair_rows, before)] * 2, (left_own, left_sib), after=(token,)
    )
    token = left[0]
    flat, chunks = [], []
    for t in range(2, n_chunk + last + 1):
        c = t - last - 1
        before_last = tuple(last_sent)
        tasks = [(j, t - LAG * j) for j in range(n_chip)]
        step([(j, i) for j, i in tasks if 0 <= i < n_chunk])
        if c < 0:
            continue
        if c == 0:
            updates += tuple(order(update_sib, owners_sib, 1))
        pins = list(before_last) if c >= 1 else []
        if c >= 1:
            pins.append(flown[c - 1][0])
        if c >= 2:
            pins.append(flown[c - 2][-1])
        push(c, pins)
        if c >= 1:
            turn(c - 1)
        if c >= 2:
            finish(c - 2)
    c = n_chunk - 1
    finish(c - 1, flown[c][:2])
    for i in range(n_chunk):
        chunks.append((offsets[i], widths[i], [len(flat) + j for j in range(n_chip)]))
        flat += own[i]
    panel_mine, panel_theirs = call(
        functools.partial(panels_kernel, chunks, n_chip, len(flat)),
        [VMEM] * len(flat),
        [VMEM] * 2,
        [f32(panel, half)] * 2,
        tuple(flat),
        after=(token,),
    )
    token = panel_mine
    early = len(cuts)
    (theirs_early,) = join(theirs_cols, [[(k, 0, anc_rows) for k in range(early)]])
    other_early = sibling(theirs_early)
    panel_other = sibling(panel_theirs)
    pieces = call(
        functools.partial(ancestor_kernel, half, cuts[:early]),
        [VMEM] * (3 + early),
        [VMEM] * (2 * early),
        [f32(anc_rows, w) for _, w in cuts[:early] * 2],
        (anc_inv, anc_rhs, *mine_cols, other_early),
        after=(token,),
    )
    token = pieces[0]
    finish(c)
    parent, solved = call(
        functools.partial(last_kernel, half, cuts, early),
        [VMEM] * (6 + 2 * early),
        [HBM] * 2,
        [f32(anc_rows, columns), f32(panel, columns)],
        (anc_inv, anc_rhs, panel_mine, panel_other, *pieces, mine_cols[-1], sibling(theirs_cols[-1])),
        after=(token,),
        scratch=[pltpu.VMEM((anc_rows, w), F32) for _, w in cuts[early:] * 2]
        + [pltpu.SemaphoreType.DMA((2 * len(cuts) + 2,))],
    )
    return (solved[None], parent[None])


def solution(mesh):
    in_specs = (
        P("leaf", "row", None),
        P("leaf", "row", None),
        P("leaf", "row", None),
        P("leaf", "row", None),
        P("leaf", "row"),
        P("leaf"),
        P("leaf", "row", None),
        P("leaf", "row", None),
    )
    out_specs = (P("leaf", "row", None), P("leaf", "row", None))
    return jax.shard_map(body, mesh=mesh, in_specs=in_specs, out_specs=out_specs, check_vma=False)
```

```python
import functools

import jax
import jax.numpy as jnp
from jax import lax
from jax.experimental import pallas as pl
from jax.experimental.pallas import tpu as pltpu
from jax.sharding import PartitionSpec as P

BLK = 128
PAIR = 2
TILE = 128
TAIL = 8
VMEM_LIMIT = 16 * 1024 * 1024
FIRST_LIMIT = 56 * 1024 * 1024
F32 = jnp.float32
BF16 = jnp.bfloat16
ANY = pl.BlockSpec(memory_space=pl.ANY)
HBM = pl.BlockSpec(memory_space=pltpu.HBM)
VMEM = pl.BlockSpec(memory_space=pltpu.VMEM)
SMEM = pl.BlockSpec(memory_space=pltpu.SMEM)


def widths_of(half):
    assert half % TILE == 0
    return [TILE // 2] * 2 + [TILE] * (half // TILE - 1)


def mxu(a, b):
    return jnp.dot(a, b, preferred_element_type=F32)


def split(x):
    high = x.astype(BF16)
    return high, (x - high.astype(F32)).astype(BF16)


def both_terms(x):
    return jnp.concatenate(split(x), axis=1)


def product(high, low, x):
    w = x.shape[1] // 2
    wide = mxu(high, x)
    return wide[:, :w] + (wide[:, w:] + mxu(low, x[:, :w]))


def times(a, b):
    return product(*split(a), both_terms(b))


def f32(*shape):
    return jax.ShapeDtypeStruct(shape, F32)


def bf16(*shape):
    return jax.ShapeDtypeStruct(shape, BF16)


def packed(rows, w):
    return (rows, TILE) if w < TILE else (PAIR * rows, w)


def put(ref, at, even, odd):
    rows, w = even.shape
    if w < TILE:
        ref[at : at + rows, :] = jnp.concatenate([even, odd], axis=1)
    else:
        ref[at : at + rows, :] = even
        ref[at + rows : at + PAIR * rows, :] = odd


def get(ref, at, rows, w):
    if w < TILE:
        both = ref[at : at + rows, :]
        return both[:, :w], both[:, w:]
    return ref[at : at + rows, :], ref[at + rows : at + PAIR * rows, :]


def call(kernel, in_specs, out_specs, out_shape, operands, after=(), scratch=(), aliases=None, limit=VMEM_LIMIT):
    n = len(operands)
    extra = len(after)

    def run(*refs):
        kernel(*refs[:n], *refs[n + extra :])

    return pl.pallas_call(
        run,
        in_specs=list(in_specs) + [ANY] * extra,
        out_specs=out_specs,
        out_shape=out_shape,
        scratch_shapes=scratch,
        input_output_aliases=aliases or {},
        compiler_params=pltpu.CompilerParams(vmem_limit_bytes=limit),
        cost_estimate=pl.CostEstimate(flops=int(10e9), bytes_accessed=1, transcendentals=0),
    )(*operands, *after)


def fetch(pairs, sems):
    copies = [pltpu.make_async_copy(a, b, sems.at[i]) for i, (a, b) in enumerate(pairs)]
    for copy in copies:
        copy.start()
    return copies


def factor_kernel(inv, inv_sib, col, col_sib, even_h, even_l, odd_h, odd_l, cross_h, cross_l):
    def fill(even, odd, cross):
        even_h[...], even_l[...] = split(even[...])
        odd_h[...], odd_l[...] = split(odd[...])
        cross_h[...], cross_l[...] = split(cross[...])

    @pl.when(lax.axis_index("row") % PAIR == 1)
    def _():
        fill(inv_sib, inv, col)

    @pl.when(lax.axis_index("row") % PAIR == 0)
    def _():
        fill(inv, inv_sib, col_sib)


def left_kernel(left, left_sib, high, low):
    panel = left.shape[0]

    def fill(even, odd):
        high[:panel, :], low[:panel, :] = split(even[...])
        high[panel:, :], low[panel:, :] = split(odd[...])

    @pl.when(lax.axis_index("row") % PAIR == 1)
    def _():
        fill(left_sib, left)

    @pl.when(lax.axis_index("row") % PAIR == 0)
    def _():
        fill(left, left_sib)


def cut_kernel(cuts, n, *refs):
    srcs, outs, sems = refs[:n], refs[n:-1], refs[-1]
    odd = lax.rem(lax.axis_index("row"), PAIR)
    pairs = []
    for (k, kind), out in zip(cuts, outs):
        w = out.shape[1]
        at = {"first": 0, "mine": odd * w, "other": (1 - odd) * w, "panel": (lax.axis_index("row") // PAIR) * PAIR * w}[kind]
        for r in range(0, out.shape[0], TILE):
            rows = pl.ds(r, TILE)
            pairs.append((srcs[k].at[rows, pl.ds(pl.multiple_of(at, TILE), w)], out.at[rows, :]))
    for copy in fetch(pairs, sems):
        copy.wait()


def block_at(place, row, n_leaf, targets_per, nblocks, leaf, owners, counts):
    dest = leaf ^ place
    source, has, slot = jnp.int32(0), jnp.int32(0), jnp.int32(-1)
    for b in range(nblocks):
        hit = (lax.div(owners[b], jnp.int32(targets_per)) == dest) & (row * nblocks + b < counts[0])
        source = jnp.where(hit, b, source)
        has = jnp.where(hit, 1, has)
        slot = jnp.where(hit, lax.rem(owners[b], jnp.int32(targets_per)), slot)
    return source, has, slot


def order_kernel(find, n_leaf, flip, owners, counts, rows, high, low, buf, sems):
    row = lax.axis_index("row") ^ flip
    found = [find(s, row, leaf=lax.axis_index("leaf"), owners=owners, counts=counts) for s in range(n_leaf)]

    def copy(s):
        at = pl.multiple_of(found[s][0] * BLK, BLK)
        return pltpu.make_async_copy(rows.at[pl.ds(at, BLK), :], buf.at[s % 4], sems.at[s % 4])

    ahead = min(3, n_leaf)
    for s in range(ahead):
        copy(s).start()
    for s in range(n_leaf):
        if s + ahead < n_leaf:
            copy(s + ahead).start()
        copy(s).wait()
        here = slice(s * BLK, (s + 1) * BLK)

        @pl.when(found[s][1] == 1)
        def _(here=here, s=s):
            high[here, :], low[here, :] = split(buf[s % 4])

        @pl.when(found[s][1] == 0)
        def _(here=here):
            high[here, :] = jnp.zeros((BLK, high.shape[1]), BF16)
            low[here, :] = jnp.zeros((BLK, high.shape[1]), BF16)


def lead_kernel(widths, *refs):
    (inv_e, inv_o, cross), refs = [refs[i : i + 2] for i in range(0, 6, 2)], refs[6:]
    rhs_own, rhs_sib, outs = refs[0], refs[1], refs[2:]
    w = sum(widths)
    odd = lax.axis_index("row") % PAIR == 1

    @pl.when(lax.axis_index("row") // PAIR == 0)
    def _():
        own, sib = rhs_own[:, :w], rhs_sib[:, :w]
        even, other = jnp.where(odd, sib, own), jnp.where(odd, own, sib)
        x_even = product(inv_e[0][...], inv_e[1][...], both_terms(even))
        other = other - product(cross[0][...], cross[1][...], both_terms(x_even))
        x_odd = product(inv_o[0][...], inv_o[1][...], both_terms(other))
        at = 0
        for part, out in zip(widths, outs):
            put(out, 0, x_even[:, at : at + part], x_odd[:, at : at + part])
            at += part


def step_kernel(tasks, n_out, *refs):
    (inv_e, inv_o, cross, left), refs = [refs[i : i + 2] for i in range(0, 8, 2)], refs[8:]
    rhs_own, rhs_sib, refs = refs[0], refs[1], refs[2:]
    outs = refs[-n_out:]
    odd = lax.axis_index("row") % PAIR == 1
    chip = lax.axis_index("row") // PAIR
    panel = rhs_own.shape[0]
    used = 0
    for stage, first, widths, which in tasks:
        known = refs[used : used + stage * len(widths)]
        used += stage * len(widths)

        @pl.when(chip == stage)
        def _(stage=stage, first=first, widths=widths, known=known, which=which):
            w = sum(widths)
            own, sib = rhs_own[:, first : first + w], rhs_sib[:, first : first + w]
            even, other = jnp.where(odd, sib, own), jnp.where(odd, own, sib)
            if stage:
                rows = []
                for i in range(stage):
                    got = [get(known[i * len(widths) + k], 0, panel, part) for k, part in enumerate(widths)]
                    rows += [jnp.concatenate([g[side] for g in got], axis=1) for side in range(PAIR)]
                x = jnp.concatenate(rows, axis=0)
                cols = slice(0, stage * PAIR * panel)
                gone = product(left[0][:, cols], left[1][:, cols], both_terms(x))
                even, other = even - gone[:panel], other - gone[panel:]
            x_even = product(inv_e[0][...], inv_e[1][...], both_terms(even))
            other = other - product(cross[0][...], cross[1][...], both_terms(x_even))
            x_odd = product(inv_o[0][...], inv_o[1][...], both_terms(other))
            at = 0
            for part, k in zip(widths, which):
                put(outs[k], 0, x_even[:, at : at + part], x_odd[:, at : at + part])
                at += part


def update_kernel(n_chip, places, w, routes, tails, find, *refs):
    if tails is not None:
        owners, owners_sib, counts, refs = refs[0], refs[1], refs[2], refs[3:]
    high, low, high_sib, low_sib = refs[:4]
    n_in = 1 + max(routes.values())
    srcs, outs, x = refs[4 : 4 + n_in], refs[4 + n_in : -1], refs[-1]
    odd = lax.axis_index("row") % PAIR == 1
    chip = lax.axis_index("row") // PAIR
    panel = x.shape[0] // (PAIR * n_chip)
    for (y, j), k in routes.items():

        @pl.when(chip == y)
        def _(j=j, src=srcs[k]):
            even, other = get(src, 0, panel, w)
            at = j * PAIR * panel
            x[at : at + panel, :] = both_terms(even)
            x[at + panel : at + PAIR * panel, :] = both_terms(other)

    n_place = len(places)
    for s in sorted(range(0, n_place, PAIR), key=lambda s: -places[s][0]):
        rows = slice(s * BLK, (s + PAIR) * BLK)
        own = product(high[rows, :], low[rows, :], x[...])
        sib = product(high_sib[rows, :], low_sib[rows, :], x[...])
        even, other = jnp.where(odd, sib, own), jnp.where(odd, own, sib)
        for i in range(PAIR):
            k, at = places[s + i]
            part = slice(i * BLK, (i + 1) * BLK)
            put(outs[k], at, even[part], other[part])
    if tails is not None:
        for s, (k, at) in enumerate(tails):
            for flip, own_list in ((0, owners), (1, owners_sib)):
                row = lax.axis_index("row") ^ flip
                _, _, slot = find(s, row, leaf=lax.axis_index("leaf"), owners=own_list, counts=counts)
                here = pl.multiple_of(at + lax.rem(row, PAIR) * TAIL, TAIL)
                outs[k][pl.ds(here, TAIL), :] = jnp.full((TAIL, TILE), slot.astype(F32))


def sum_kernel(blocks, tail, w, n_src, merge, *refs):
    if tail is None:
        slots, refs = refs[0], refs[1:]
    srcs, refs = refs[:n_src], refs[n_src:]
    if merge:
        old_mine, old_theirs, refs = refs[0], refs[1], refs[2:]
    if tail is None:
        mine, theirs, total = refs
    else:
        mine, theirs, slots, total = refs
        for s, (k, at) in enumerate(blocks):
            for i in range(PAIR):
                here = slice(at + tail + i * TAIL, at + tail + (i + 1) * TAIL)
                slots[PAIR * s + i] = jnp.max(srcs[k][here, :]).astype(jnp.int32)
    odd = lax.axis_index("row") % PAIR == 1
    total[...] = jnp.zeros_like(total)
    for s, (k, at) in enumerate(blocks):
        got = get(srcs[k], at, BLK, w)
        for i in range(PAIR):
            slot = slots[PAIR * s + i]

            @pl.when(slot >= 0)
            def _(slot=slot, i=i, got=got):
                place = pl.ds(pl.multiple_of(slot * BLK, BLK), BLK)
                total[i, place, :] += got[i]

    a = jnp.where(odd, total[1], total[0])
    b = jnp.where(odd, total[0], total[1])
    if merge:
        a = jnp.concatenate([old_mine[...], a], axis=1)
        b = jnp.concatenate([old_theirs[...], b], axis=1)
    mine[...] = a
    theirs[...] = b


def solve_blocks(inv, rhs, at, total, put_rows):
    w = total.shape[1]
    for t in range(total.shape[0] // BLK):
        rows = slice(t * BLK, (t + 1) * BLK)
        put_rows(rows, times(inv[rows, :], rhs[rows, pl.ds(at, w)] - total[rows, :]))


def ancestor_kernel(half, cuts, inv, rhs, *refs):
    n = len(cuts)
    mine, other, outs = refs[:n], refs[n], refs[n + 1 :]
    odd = lax.rem(lax.axis_index("row"), PAIR)
    rows_all = inv.shape[0]
    for k, (first, _) in enumerate(cuts):
        for side, total, out in (
            (odd, mine[k], outs[k]),
            (1 - odd, other.at[k * rows_all : (k + 1) * rows_all, :], outs[n + k]),
        ):

            def put_rows(rows, x, out=out):
                out[rows, :] = x

            solve_blocks(inv, rhs, pl.multiple_of(side * half + first, TILE), total, put_rows)


def last_kernel(half, cuts, n_early, inv, rhs, panel_mine, panel_other, *refs):
    n = len(cuts)
    pieces, totals, out, solved = refs[: 2 * n_early], refs[2 * n_early : 2 * n], refs[2 * n], refs[2 * n + 1]
    scratch, sems = refs[2 * n + 2 : -1], refs[-1]
    odd = lax.rem(lax.axis_index("row"), PAIR)
    copies = []

    def send(src, dst, mine, first, w):
        at = pl.multiple_of((odd if mine else 1 - odd) * half + first, TILE)
        copy = pltpu.make_async_copy(src, dst.at[:, pl.ds(at, w)], sems.at[len(copies)])
        copy.start()
        copies.append(copy)

    for i in range(2 * n_early):
        send(pieces[i], out, i < n_early, *cuts[i % n_early])
    send(panel_mine, solved, True, 0, half)
    send(panel_other, solved, False, 0, half)
    late = n - n_early
    for i in range(2 * late):
        first, w = cuts[n_early + i % late]
        at = pl.multiple_of((odd if i < late else 1 - odd) * half + first, TILE)

        def put_rows(rows, x, buf=scratch[i]):
            buf[rows, :] = x

        solve_blocks(inv, rhs, at, totals[i], put_rows)
        send(scratch[i], out, i < late, first, w)
    for copy in copies:
        copy.wait()


def panels_kernel(chunks, n_chip, n_src, *refs):
    srcs, mine, theirs = refs[:n_src], refs[-2], refs[-1]
    odd = lax.axis_index("row") % PAIR == 1
    chip = lax.axis_index("row") // PAIR
    panel = mine.shape[0]
    for first, w, ks in chunks:
        for j in range(n_chip):

            @pl.when(chip == j)
            def _(src=srcs[ks[j]], first=first, w=w):
                even, other = get(src, 0, panel, w)
                mine[:, first : first + w] = jnp.where(odd, other, even)
                theirs[:, first : first + w] = jnp.where(odd, even, other)


def join_kernel(cuts, n, *refs):
    srcs, outs = refs[:n], refs[n:]
    for out, parts in zip(outs, cuts):
        at = 0
        for k, first, count in parts:
            out[at : at + count, :] = srcs[k][first : first + count, :]
            at += count


def body(
    right_side,
    lower_rows,
    diag_inverse,
    update_rows,
    owner_map,
    block_counts,
    ancestor_rhs,
    ancestor_inverse,
):
    n_row = lax.axis_size("row")
    n_leaf = lax.axis_size("leaf")
    my_row = lax.axis_index("row")
    my_leaf = lax.axis_index("leaf")
    side = my_row % PAIR
    n_chip = n_row // PAIR
    chip = my_row // PAIR
    rhs = right_side[0]
    lower = lower_rows[0]
    inverse = diag_inverse[0]
    update = update_rows[0]
    owners = owner_map[0]
    panel, columns = rhs.shape
    pair_rows = PAIR * panel
    half = columns // PAIR
    piv = update.shape[1]
    nblocks = update.shape[0] // BLK
    anc_rhs = ancestor_rhs[0]
    anc_inv = ancestor_inverse[0]
    anc_rows = anc_rhs.shape[0]
    targets_per = anc_rows // BLK

    widths = widths_of(half)
    offsets = [sum(widths[:i]) for i in range(len(widths))]
    n_chunk = len(widths)

    swap = [(r, r ^ 1) for r in range(n_row)]

    def sibling(a):
        return lax.ppermute(a, "row", swap)

    def across(a, mask):
        return lax.ppermute(a, "leaf", [(i, i ^ mask) for i in range(n_leaf)])

    def cut(arrays, cuts, after=(), limit=VMEM_LIMIT):
        return call(
            functools.partial(cut_kernel, [c[:2] for c in cuts], len(arrays)),
            [HBM] * len(arrays),
            [VMEM] * len(cuts),
            [f32(arrays[k].shape[0], w) for k, _, w in cuts],
            tuple(arrays),
            after=after,
            scratch=[pltpu.SemaphoreType.DMA((sum(arrays[k].shape[0] // TILE for k, _, _ in cuts),))],
            limit=limit,
        )

    col, rhs_own, rhs_out = cut([lower, rhs], [(0, "panel", panel), (1, "mine", half), (1, "other", half)], limit=FIRST_LIMIT)
    inv_sib = sibling(inverse)
    col_sib = sibling(col)
    rhs_sib = sibling(rhs_out)
    owners_sib = sibling(owners)
    before = max((n_chip - 1) * pair_rows, panel)

    factors = call(
        factor_kernel,
        [VMEM] * 4,
        [VMEM] * 6,
        [bf16(panel, panel)] * 6,
        (inverse, inv_sib, col, col_sib),
        after=(rhs_sib, owners_sib),
    )
    token = factors[0]
    left = None

    own = [[None] * n_chip for _ in range(n_chunk)]
    there = [[None] * n_chip for _ in range(n_chunk)]
    last_sent = []

    def step(tasks, after=()):
        nonlocal token, last_sent
        if not tasks:
            return
        kinds, places = [], []
        for j, cs in tasks:
            place = []
            for c in cs:
                k = next((k for k, (w, js) in enumerate(kinds) if w == widths[c] and j not in js), len(kinds))
                if k == len(kinds):
                    kinds.append((widths[c], {}))
                kinds[k][1][j] = c
                place.append(k)
            places.append(place)
        known = [there[c][i][(j - i) % n_chip] for j, cs in tasks for i in range(j) for c in cs]
        lefts = left if left is not None else factors[4:6]
        plan = [(j, offsets[cs[0]], [widths[c] for c in cs], place) for (j, cs), place in zip(tasks, places)]
        outs = call(
            functools.partial(step_kernel, plan, len(kinds)),
            [VMEM] * (10 + len(known)),
            [VMEM] * len(kinds),
            [f32(*packed(panel, w)) for w, _ in kinds],
            (*factors, *lefts, rhs_own, rhs_sib, *known),
            after=(token, *after),
        )
        token = outs[0]
        last_sent = []
        for (w, here), out in zip(kinds, outs):
            got = {}
            for k in range(1, n_chip):
                perm = []
                for j in here:
                    to = (j + k) % n_chip
                    perm += [(PAIR * j + i, PAIR * to + i) for i in range(PAIR)]
                got[k] = lax.ppermute(out, "row", perm)
                last_sent.append(got[k])
            for j, c in here.items():
                own[c][j] = out
                there[c][j] = got

    def lead(n):
        nonlocal token
        outs = call(
            functools.partial(lead_kernel, widths[:n]),
            [VMEM] * 8,
            [VMEM] * n,
            [f32(*packed(panel, w)) for w in widths[:n]],
            (*factors, rhs_own, rhs_sib),
            after=(token,),
        )
        token = outs[0]
        for c, out in enumerate(outs):
            got = {}
            for k in range(1, n_chip):
                got[k] = lax.ppermute(out, "row", [(i, PAIR * k + i) for i in range(PAIR)])
            own[c][0] = out
            there[c][0] = got

    find = functools.partial(block_at, n_leaf=n_leaf, targets_per=targets_per, nblocks=nblocks)

    def order(rows, own_list, flip):
        nonlocal token
        outs = call(
            functools.partial(order_kernel, find, n_leaf, flip),
            [SMEM] * 2 + [HBM],
            [VMEM] * 2,
            [bf16(n_leaf * BLK, piv)] * 2,
            (own_list, block_counts, rows),
            after=(token,),
            scratch=[pltpu.VMEM((4, BLK, piv), F32), pltpu.SemaphoreType.DMA((4,))],
        )
        token = outs[0]
        return outs

    def join(arrays, cuts):
        nonlocal token
        outs = call(
            functools.partial(join_kernel, cuts, len(arrays)),
            [VMEM] * len(arrays),
            [VMEM] * len(cuts),
            [f32(sum(p[2] for p in parts), TILE) for parts in cuts],
            arrays,
            after=(token,),
        )
        token = outs[0]
        return outs

    far = sorted(range(2, n_leaf, 2), key=lambda m: (m & -m) * 2 * n_leaf - m, reverse=True)
    held, flown = {}, {}
    updates = ()

    def unit(c):
        return packed(BLK, widths[c])[0] + (PAIR * TAIL if c == 0 else 0)

    def fly(c, sends):
        flown.setdefault(c, [])
        for m, a, qs in sends:
            got = lax.ppermute(a, "leaf", [(i, i ^ m) for i in range(n_leaf)])
            flown[c].append(got)
            held[c] += [(got, i * unit(c), q ^ m, first) for i, (q, first) in enumerate(qs)]

    def push(c, after=()):
        nonlocal token
        w = widths[c]
        n = unit(c)
        if c + 1 < n_chunk:
            groups = [(0, [0, 1])] + [(m, [m, m + 1]) for m in far]
        else:
            groups = [(0, list(range(0, n_leaf, 2))), (1, list(range(1, n_leaf, 2)))]
        spots = {q: (k, i * n) for k, (_, qs) in enumerate(groups) for i, q in enumerate(qs)}
        places = [spots[q] for q in range(n_leaf)]
        tails = [(k, at + packed(BLK, w)[0]) for k, at in places] if c == 0 else None
        arrays, routes = [], {}
        for y in range(n_chip):
            for j in range(n_chip):
                a = own[c][j] if y == j else there[c][j][(y - j) % n_chip]
                k = next((k for k, b in enumerate(arrays) if b is a), len(arrays))
                if k == len(arrays):
                    arrays.append(a)
                routes[y, j] = k
        maps = (owners, owners_sib, block_counts) if c == 0 else ()
        outs = call(
            functools.partial(update_kernel, n_chip, places, w, routes, tails, find),
            [SMEM] * len(maps) + [VMEM] * (4 + len(arrays)),
            [VMEM] * len(groups),
            [f32(len(qs) * n, TILE) for _, qs in groups],
            (*maps, *updates, *arrays),
            after=(token, *after),
            scratch=[pltpu.VMEM((piv, 2 * w), BF16)],
        )
        token = outs[0]
        held[c] = [(outs[0], i * n, q, q) for i, q in enumerate(groups[0][1])]
        fly(c, [(m, a, [(q, q) for q in qs]) for (m, qs), a in zip(groups[1:], outs[1:])])

    def turn(c, after=()):
        nonlocal token
        n = unit(c)
        masks = [1] if c + 1 < n_chunk else far
        arrays, cuts, going = [], [], []
        for m in masks:
            parts, qs = [], []
            for a, at, q, first in held[c]:
                if q == m:
                    k = next((k for k, b in enumerate(arrays) if b is a), len(arrays))
                    if k == len(arrays):
                        arrays.append(a)
                    parts.append((k, at, n))
                    qs.append((q, first))
            cuts.append(parts)
            going.append(qs)
        held[c] = [b for b in held[c] if b[2] == 0]
        fly(c, list(zip(masks, join(arrays, cuts, after), going)))

    def join(arrays, cuts, after=()):
        nonlocal token
        outs = call(
            functools.partial(join_kernel, cuts, len(arrays)),
            [VMEM] * len(arrays),
            [VMEM] * len(cuts),
            [f32(sum(p[2] for p in parts), TILE) for parts in cuts],
            arrays,
            after=(token, *after),
        )
        token = outs[0]
        return outs

    slots = None
    mine_cols, theirs_cols, cuts = [], [], []
    carry = None

    def finish(c, after=()):
        nonlocal token, slots, carry
        w = widths[c]
        arrays, blocks = [], []
        for a, at, _, _ in sorted(held[c], key=lambda b: b[3]):
            k = next((k for k, b in enumerate(arrays) if b is a), len(arrays))
            if k == len(arrays):
                arrays.append(a)
            blocks.append((k, at))
        tail = packed(BLK, w)[0] if c == 0 else None
        lookup = () if c == 0 else tuple(slots)
        merge = carry is not None
        hold = w < TILE and not merge
        shape = f32(anc_rows, 2 * w if merge else w)
        outs = call(
            functools.partial(sum_kernel, blocks, tail, w, len(arrays), merge),
            [SMEM] * len(lookup) + [VMEM] * (len(arrays) + (2 if merge else 0)),
            [VMEM] * 2 + ([SMEM] if c == 0 else []),
            [shape] * 2 + ([jax.ShapeDtypeStruct((n_leaf * PAIR,), jnp.int32)] if c == 0 else []),
            (*lookup, *arrays, *(carry or ())),
            after=(token, *after),
            scratch=[pltpu.VMEM((PAIR, anc_rows, w), F32)],
        )
        token = outs[0]
        if c == 0:
            slots = outs[2:]
        if hold:
            carry = (outs[0], outs[1])
            return
        carry = None
        mine_cols.append(outs[0])
        theirs_cols.append(outs[1])
        cuts.append((offsets[c] + w - shape.shape[1], shape.shape[1]))

    left_own = lower[:, :before]
    left_sib = sibling(lax.optimization_barrier((left_own, token))[0])
    lead(2)
    update_sib = sibling(lax.optimization_barrier((update, token))[0])
    updates = tuple(order(update, owners, 0))
    left = call(
        left_kernel, [VMEM] * 2, [VMEM] * 2, [bf16(pair_rows, before)] * 2, (left_own, left_sib), after=(token,)
    )
    token = left[0]
    stages = range(1, n_chip)
    for j in stages:
        step([(j, (0, 1))] + ([(0, (2, 3)[: n_chunk - 2])] if j == 1 else []))
    updates += tuple(order(update_sib, owners_sib, 1))
    push(0)
    push(1)
    for c in range(2, n_chunk + 1):
        before_last = list(last_sent)
        for j in stages:
            if c < n_chunk:
                step([(j, (c,))] + ([(0, (c + 2,))] if j == 1 and c + 2 < n_chunk else []))
        if c > 2:
            push(c - 1)
        turn(c - 2)
        if c == n_chunk:
            turn(c - 1)
        if c > 2:
            finish(c - 3)
    c = n_chunk - 1
    flat, chunks = [], []
    for i in range(n_chunk):
        chunks.append((offsets[i], widths[i], [len(flat) + j for j in range(n_chip)]))
        flat += own[i]
    panel_mine, panel_theirs = call(
        functools.partial(panels_kernel, chunks, n_chip, len(flat)),
        [VMEM] * len(flat),
        [VMEM] * 2,
        [f32(panel, half)] * 2,
        tuple(flat),
        after=(token,),
    )
    token = panel_mine
    early = len(cuts)
    (theirs_early,) = join(theirs_cols, [[(k, 0, anc_rows) for k in range(early)]])
    other_early = sibling(theirs_early)
    panel_other = sibling(panel_theirs)
    finish(c)
    finish(c - 1)
    pieces = call(
        functools.partial(ancestor_kernel, half, cuts[:early]),
        [VMEM] * (3 + early),
        [VMEM] * (2 * early),
        [f32(anc_rows, w) for _, w in cuts[:early] * 2],
        (anc_inv, anc_rhs, *mine_cols[:early], other_early),
        after=(token,),
    )
    token = pieces[0]
    late = [sibling(a) for a in theirs_cols[early:]]
    parent, solved = call(
        functools.partial(last_kernel, half, cuts, early),
        [VMEM] * (4 + 2 * len(cuts)),
        [HBM] * 2,
        [f32(anc_rows, columns), f32(panel, columns)],
        (anc_inv, anc_rhs, panel_mine, panel_other, *pieces, *mine_cols[early:], *late),
        after=(token,),
        scratch=[pltpu.VMEM((anc_rows, w), F32) for _, w in cuts[early:] * 2]
        + [pltpu.SemaphoreType.DMA((2 * len(cuts) + 2,))],
    )
    return (solved[None], parent[None])


def solution(mesh):
    in_specs = (
        P("leaf", "row", None),
        P("leaf", "row", None),
        P("leaf", "row", None),
        P("leaf", "row", None),
        P("leaf", "row"),
        P("leaf"),
        P("leaf", "row", None),
        P("leaf", "row", None),
    )
    out_specs = (P("leaf", "row", None), P("leaf", "row", None))
    return jax.shard_map(body, mesh=mesh, in_specs=in_specs, out_specs=out_specs, check_vma=False)
```

```python
import functools

import jax
import jax.numpy as jnp
from jax import lax
from jax.experimental import pallas as pl
from jax.experimental.pallas import tpu as pltpu
from jax.sharding import PartitionSpec as P

BLK = 128
PAIR = 2
TILE = 128
TAIL = 8
VMEM_LIMIT = 16 * 1024 * 1024
FIRST_LIMIT = 56 * 1024 * 1024
F32 = jnp.float32
BF16 = jnp.bfloat16
ANY = pl.BlockSpec(memory_space=pl.ANY)
HBM = pl.BlockSpec(memory_space=pltpu.HBM)
VMEM = pl.BlockSpec(memory_space=pltpu.VMEM)
SMEM = pl.BlockSpec(memory_space=pltpu.SMEM)


def widths_of(half):
    assert half % TILE == 0
    return [TILE // 2] * 2 + [TILE] * (half // TILE - 1)


def mxu(a, b):
    return jnp.dot(a, b, preferred_element_type=F32)


def split(x):
    high = x.astype(BF16)
    return high, (x - high.astype(F32)).astype(BF16)


def both_terms(x):
    return jnp.concatenate(split(x), axis=1)


def product(high, low, x):
    w = x.shape[1] // 2
    wide = mxu(high, x)
    return wide[:, :w] + (wide[:, w:] + mxu(low, x[:, :w]))


def times(a, b):
    return product(*split(a), both_terms(b))


def f32(*shape):
    return jax.ShapeDtypeStruct(shape, F32)


def bf16(*shape):
    return jax.ShapeDtypeStruct(shape, BF16)


def packed(rows, w):
    return (rows, TILE) if w < TILE else (PAIR * rows, w)


def put(ref, at, even, odd):
    rows, w = even.shape
    if w < TILE:
        ref[at : at + rows, :] = jnp.concatenate([even, odd], axis=1)
    else:
        ref[at : at + rows, :] = even
        ref[at + rows : at + PAIR * rows, :] = odd


def get(ref, at, rows, w):
    if w < TILE:
        both = ref[at : at + rows, :]
        return both[:, :w], both[:, w:]
    return ref[at : at + rows, :], ref[at + rows : at + PAIR * rows, :]


def call(kernel, in_specs, out_specs, out_shape, operands, after=(), scratch=(), aliases=None, limit=VMEM_LIMIT):
    n = len(operands)
    extra = len(after)

    def run(*refs):
        kernel(*refs[:n], *refs[n + extra :])

    return pl.pallas_call(
        run,
        in_specs=list(in_specs) + [ANY] * extra,
        out_specs=out_specs,
        out_shape=out_shape,
        scratch_shapes=scratch,
        input_output_aliases=aliases or {},
        compiler_params=pltpu.CompilerParams(vmem_limit_bytes=limit),
        cost_estimate=pl.CostEstimate(flops=int(10e9), bytes_accessed=1, transcendentals=0),
    )(*operands, *after)


def fetch(pairs, sems):
    copies = [pltpu.make_async_copy(a, b, sems.at[i]) for i, (a, b) in enumerate(pairs)]
    for copy in copies:
        copy.start()
    return copies


def factor_kernel(inv, inv_sib, col, col_sib, even_h, even_l, odd_h, odd_l, cross_h, cross_l):
    def fill(even, odd, cross):
        even_h[...], even_l[...] = split(even[...])
        odd_h[...], odd_l[...] = split(odd[...])
        cross_h[...], cross_l[...] = split(cross[...])

    @pl.when(lax.axis_index("row") % PAIR == 1)
    def _():
        fill(inv_sib, inv, col)

    @pl.when(lax.axis_index("row") % PAIR == 0)
    def _():
        fill(inv, inv_sib, col_sib)


def left_kernel(left, left_sib, high, low):
    panel = left.shape[0]

    def fill(even, odd):
        high[:panel, :], low[:panel, :] = split(even[...])
        high[panel:, :], low[panel:, :] = split(odd[...])

    @pl.when(lax.axis_index("row") % PAIR == 1)
    def _():
        fill(left_sib, left)

    @pl.when(lax.axis_index("row") % PAIR == 0)
    def _():
        fill(left, left_sib)


def cut_kernel(cuts, n, *refs):
    srcs, outs, sems = refs[:n], refs[n:-1], refs[-1]
    odd = lax.rem(lax.axis_index("row"), PAIR)
    pairs = []
    for (k, kind), out in zip(cuts, outs):
        w = out.shape[1]
        at = {"first": 0, "mine": odd * w, "other": (1 - odd) * w, "panel": (lax.axis_index("row") // PAIR) * PAIR * w}[kind]
        for r in range(0, out.shape[0], TILE):
            rows = pl.ds(r, TILE)
            pairs.append((srcs[k].at[rows, pl.ds(pl.multiple_of(at, TILE), w)], out.at[rows, :]))
    for copy in fetch(pairs, sems):
        copy.wait()


def block_at(place, row, n_leaf, targets_per, nblocks, leaf, owners, counts):
    dest = leaf ^ place
    source, has, slot = jnp.int32(0), jnp.int32(0), jnp.int32(-1)
    for b in range(nblocks):
        hit = (lax.div(owners[b], jnp.int32(targets_per)) == dest) & (row * nblocks + b < counts[0])
        source = jnp.where(hit, b, source)
        has = jnp.where(hit, 1, has)
        slot = jnp.where(hit, lax.rem(owners[b], jnp.int32(targets_per)), slot)
    return source, has, slot


def order_kernel(find, n_leaf, flip, owners, counts, rows, high, low, buf, sems):
    row = lax.axis_index("row") ^ flip
    found = [find(s, row, leaf=lax.axis_index("leaf"), owners=owners, counts=counts) for s in range(n_leaf)]

    def copy(s):
        at = pl.multiple_of(found[s][0] * BLK, BLK)
        return pltpu.make_async_copy(rows.at[pl.ds(at, BLK), :], buf.at[s % 4], sems.at[s % 4])

    ahead = min(3, n_leaf)
    for s in range(ahead):
        copy(s).start()
    for s in range(n_leaf):
        if s + ahead < n_leaf:
            copy(s + ahead).start()
        copy(s).wait()
        here = slice(s * BLK, (s + 1) * BLK)

        @pl.when(found[s][1] == 1)
        def _(here=here, s=s):
            high[here, :], low[here, :] = split(buf[s % 4])

        @pl.when(found[s][1] == 0)
        def _(here=here):
            high[here, :] = jnp.zeros((BLK, high.shape[1]), BF16)
            low[here, :] = jnp.zeros((BLK, high.shape[1]), BF16)


def lead_kernel(widths, *refs):
    (inv_e, inv_o, cross), refs = [refs[i : i + 2] for i in range(0, 6, 2)], refs[6:]
    rhs_own, rhs_sib, outs = refs[0], refs[1], refs[2:]
    w = sum(widths)
    odd = lax.axis_index("row") % PAIR == 1

    @pl.when(lax.axis_index("row") // PAIR == 0)
    def _():
        own, sib = rhs_own[:, :w], rhs_sib[:, :w]
        even, other = jnp.where(odd, sib, own), jnp.where(odd, own, sib)
        x_even = product(inv_e[0][...], inv_e[1][...], both_terms(even))
        other = other - product(cross[0][...], cross[1][...], both_terms(x_even))
        x_odd = product(inv_o[0][...], inv_o[1][...], both_terms(other))
        at = 0
        for part, out in zip(widths, outs):
            put(out, 0, x_even[:, at : at + part], x_odd[:, at : at + part])
            at += part


def step_kernel(tasks, n_out, *refs):
    (inv_e, inv_o, cross, left), refs = [refs[i : i + 2] for i in range(0, 8, 2)], refs[8:]
    rhs_own, rhs_sib, refs = refs[0], refs[1], refs[2:]
    outs = refs[-n_out:]
    odd = lax.axis_index("row") % PAIR == 1
    chip = lax.axis_index("row") // PAIR
    panel = rhs_own.shape[0]
    used = 0
    for stage, first, widths, which in tasks:
        known = refs[used : used + stage * len(widths)]
        used += stage * len(widths)

        @pl.when(chip == stage)
        def _(stage=stage, first=first, widths=widths, known=known, which=which):
            w = sum(widths)
            own, sib = rhs_own[:, first : first + w], rhs_sib[:, first : first + w]
            even, other = jnp.where(odd, sib, own), jnp.where(odd, own, sib)
            if stage:
                rows = []
                for i in range(stage):
                    got = [get(known[i * len(widths) + k], 0, panel, part) for k, part in enumerate(widths)]
                    rows += [jnp.concatenate([g[side] for g in got], axis=1) for side in range(PAIR)]
                x = jnp.concatenate(rows, axis=0)
                cols = slice(0, stage * PAIR * panel)
                gone = product(left[0][:, cols], left[1][:, cols], both_terms(x))
                even, other = even - gone[:panel], other - gone[panel:]
            x_even = product(inv_e[0][...], inv_e[1][...], both_terms(even))
            other = other - product(cross[0][...], cross[1][...], both_terms(x_even))
            x_odd = product(inv_o[0][...], inv_o[1][...], both_terms(other))
            at = 0
            for part, k in zip(widths, which):
                put(outs[k], 0, x_even[:, at : at + part], x_odd[:, at : at + part])
                at += part


def update_kernel(n_chip, places, w, routes, tails, find, *refs):
    if tails is not None:
        owners, owners_sib, counts, refs = refs[0], refs[1], refs[2], refs[3:]
    high, low, high_sib, low_sib = refs[:4]
    n_in = 1 + max(routes.values())
    srcs, outs, x = refs[4 : 4 + n_in], refs[4 + n_in : -1], refs[-1]
    odd = lax.axis_index("row") % PAIR == 1
    chip = lax.axis_index("row") // PAIR
    panel = x.shape[0] // (PAIR * n_chip)
    for (y, j), k in routes.items():

        @pl.when(chip == y)
        def _(j=j, src=srcs[k]):
            even, other = get(src, 0, panel, w)
            at = j * PAIR * panel
            x[at : at + panel, :] = both_terms(even)
            x[at + panel : at + PAIR * panel, :] = both_terms(other)

    n_place = len(places)
    for s in sorted(range(0, n_place, PAIR), key=lambda s: -places[s][0]):
        rows = slice(s * BLK, (s + PAIR) * BLK)
        own = product(high[rows, :], low[rows, :], x[...])
        sib = product(high_sib[rows, :], low_sib[rows, :], x[...])
        even, other = jnp.where(odd, sib, own), jnp.where(odd, own, sib)
        for i in range(PAIR):
            k, at = places[s + i]
            part = slice(i * BLK, (i + 1) * BLK)
            put(outs[k], at, even[part], other[part])
    if tails is not None:
        for s, (k, at) in enumerate(tails):
            for flip, own_list in ((0, owners), (1, owners_sib)):
                row = lax.axis_index("row") ^ flip
                _, _, slot = find(s, row, leaf=lax.axis_index("leaf"), owners=own_list, counts=counts)
                here = pl.multiple_of(at + lax.rem(row, PAIR) * TAIL, TAIL)
                outs[k][pl.ds(here, TAIL), :] = jnp.full((TAIL, TILE), slot.astype(F32))


def sum_kernel(blocks, tail, w, n_src, merge, *refs):
    if tail is None:
        slots, refs = refs[0], refs[1:]
    srcs, refs = refs[:n_src], refs[n_src:]
    if merge:
        old_mine, old_theirs, refs = refs[0], refs[1], refs[2:]
    if tail is None:
        mine, theirs, total = refs
    else:
        mine, theirs, slots, total = refs
        for s, (k, at) in enumerate(blocks):
            for i in range(PAIR):
                here = slice(at + tail + i * TAIL, at + tail + (i + 1) * TAIL)
                slots[PAIR * s + i] = jnp.max(srcs[k][here, :]).astype(jnp.int32)
    odd = lax.axis_index("row") % PAIR == 1
    total[...] = jnp.zeros_like(total)
    for s, (k, at) in enumerate(blocks):
        got = get(srcs[k], at, BLK, w)
        for i in range(PAIR):
            slot = slots[PAIR * s + i]

            @pl.when(slot >= 0)
            def _(slot=slot, i=i, got=got):
                place = pl.ds(pl.multiple_of(slot * BLK, BLK), BLK)
                total[i, place, :] += got[i]

    a = jnp.where(odd, total[1], total[0])
    b = jnp.where(odd, total[0], total[1])
    if merge:
        a = jnp.concatenate([old_mine[...], a], axis=1)
        b = jnp.concatenate([old_theirs[...], b], axis=1)
    mine[...] = a
    theirs[...] = b


def solve_blocks(inv, rhs, at, total, put_rows):
    w = total.shape[1]
    for t in range(total.shape[0] // BLK):
        rows = slice(t * BLK, (t + 1) * BLK)
        put_rows(rows, times(inv[rows, :], rhs[rows, pl.ds(at, w)] - total[rows, :]))


def ancestor_kernel(half, cuts, inv, rhs, *refs):
    n = len(cuts)
    mine, other, outs = refs[:n], refs[n], refs[n + 1 :]
    odd = lax.rem(lax.axis_index("row"), PAIR)
    rows_all = inv.shape[0]
    for k, (first, _) in enumerate(cuts):
        for side, total, out in (
            (odd, mine[k], outs[k]),
            (1 - odd, other.at[k * rows_all : (k + 1) * rows_all, :], outs[n + k]),
        ):

            def put_rows(rows, x, out=out):
                out[rows, :] = x

            solve_blocks(inv, rhs, pl.multiple_of(side * half + first, TILE), total, put_rows)


def last_kernel(half, cuts, n_early, inv, rhs, panel_mine, panel_other, *refs):
    n = len(cuts)
    pieces, totals, out, solved = refs[: 2 * n_early], refs[2 * n_early : 2 * n], refs[2 * n], refs[2 * n + 1]
    scratch, sems = refs[2 * n + 2 : -1], refs[-1]
    odd = lax.rem(lax.axis_index("row"), PAIR)
    copies = []

    def send(src, dst, mine, first, w):
        at = pl.multiple_of((odd if mine else 1 - odd) * half + first, TILE)
        copy = pltpu.make_async_copy(src, dst.at[:, pl.ds(at, w)], sems.at[len(copies)])
        copy.start()
        copies.append(copy)

    for i in range(2 * n_early):
        send(pieces[i], out, i < n_early, *cuts[i % n_early])
    send(panel_mine, solved, True, 0, half)
    send(panel_other, solved, False, 0, half)
    late = n - n_early
    for i in range(2 * late):
        first, w = cuts[n_early + i % late]
        at = pl.multiple_of((odd if i < late else 1 - odd) * half + first, TILE)

        def put_rows(rows, x, buf=scratch[i]):
            buf[rows, :] = x

        solve_blocks(inv, rhs, at, totals[i], put_rows)
        send(scratch[i], out, i < late, first, w)
    for copy in copies:
        copy.wait()


def panels_kernel(chunks, n_chip, n_src, *refs):
    srcs, mine, theirs = refs[:n_src], refs[-2], refs[-1]
    odd = lax.axis_index("row") % PAIR == 1
    chip = lax.axis_index("row") // PAIR
    panel = mine.shape[0]
    for first, w, ks in chunks:
        for j in range(n_chip):

            @pl.when(chip == j)
            def _(src=srcs[ks[j]], first=first, w=w):
                even, other = get(src, 0, panel, w)
                mine[:, first : first + w] = jnp.where(odd, other, even)
                theirs[:, first : first + w] = jnp.where(odd, even, other)


def join_kernel(cuts, n, *refs):
    srcs, outs = refs[:n], refs[n:]
    for out, parts in zip(outs, cuts):
        at = 0
        for k, first, count in parts:
            out[at : at + count, :] = srcs[k][first : first + count, :]
            at += count


def body(
    right_side,
    lower_rows,
    diag_inverse,
    update_rows,
    owner_map,
    block_counts,
    ancestor_rhs,
    ancestor_inverse,
):
    n_row = lax.axis_size("row")
    n_leaf = lax.axis_size("leaf")
    my_row = lax.axis_index("row")
    my_leaf = lax.axis_index("leaf")
    side = my_row % PAIR
    n_chip = n_row // PAIR
    chip = my_row // PAIR
    rhs = right_side[0]
    lower = lower_rows[0]
    inverse = diag_inverse[0]
    update = update_rows[0]
    owners = owner_map[0]
    panel, columns = rhs.shape
    pair_rows = PAIR * panel
    half = columns // PAIR
    piv = update.shape[1]
    nblocks = update.shape[0] // BLK
    anc_rhs = ancestor_rhs[0]
    anc_inv = ancestor_inverse[0]
    anc_rows = anc_rhs.shape[0]
    targets_per = anc_rows // BLK

    widths = widths_of(half)
    offsets = [sum(widths[:i]) for i in range(len(widths))]
    n_chunk = len(widths)

    swap = [(r, r ^ 1) for r in range(n_row)]

    def sibling(a):
        return lax.ppermute(a, "row", swap)

    def across(a, mask):
        return lax.ppermute(a, "leaf", [(i, i ^ mask) for i in range(n_leaf)])

    def cut(arrays, cuts, after=(), limit=VMEM_LIMIT):
        return call(
            functools.partial(cut_kernel, [c[:2] for c in cuts], len(arrays)),
            [HBM] * len(arrays),
            [VMEM] * len(cuts),
            [f32(arrays[k].shape[0], w) for k, _, w in cuts],
            tuple(arrays),
            after=after,
            scratch=[pltpu.SemaphoreType.DMA((sum(arrays[k].shape[0] // TILE for k, _, _ in cuts),))],
            limit=limit,
        )

    col, rhs_own, rhs_out = cut([lower, rhs], [(0, "panel", panel), (1, "mine", half), (1, "other", half)], limit=FIRST_LIMIT)
    inv_sib = sibling(inverse)
    col_sib = sibling(col)
    rhs_sib = sibling(rhs_out)
    owners_sib = sibling(owners)
    before = max((n_chip - 1) * pair_rows, panel)

    factors = call(
        factor_kernel,
        [VMEM] * 4,
        [VMEM] * 6,
        [bf16(panel, panel)] * 6,
        (inverse, inv_sib, col, col_sib),
        after=(rhs_sib, owners_sib),
    )
    token = factors[0]
    left = None

    own = [[None] * n_chip for _ in range(n_chunk)]
    there = [[None] * n_chip for _ in range(n_chunk)]
    last_sent = []

    def step(tasks, after=()):
        nonlocal token, last_sent
        if not tasks:
            return
        kinds, places = [], []
        for j, cs in tasks:
            place = []
            for c in cs:
                k = next((k for k, (w, js) in enumerate(kinds) if w == widths[c] and j not in js), len(kinds))
                if k == len(kinds):
                    kinds.append((widths[c], {}))
                kinds[k][1][j] = c
                place.append(k)
            places.append(place)
        known = [there[c][i][(j - i) % n_chip] for j, cs in tasks for i in range(j) for c in cs]
        lefts = left if left is not None else factors[4:6]
        plan = [(j, offsets[cs[0]], [widths[c] for c in cs], place) for (j, cs), place in zip(tasks, places)]
        outs = call(
            functools.partial(step_kernel, plan, len(kinds)),
            [VMEM] * (10 + len(known)),
            [VMEM] * len(kinds),
            [f32(*packed(panel, w)) for w, _ in kinds],
            (*factors, *lefts, rhs_own, rhs_sib, *known),
            after=(token, *after),
        )
        token = outs[0]
        last_sent = []
        for (w, here), out in zip(kinds, outs):
            got = {}
            for k in range(1, n_chip):
                perm = []
                for j in here:
                    to = (j + k) % n_chip
                    perm += [(PAIR * j + i, PAIR * to + i) for i in range(PAIR)]
                got[k] = lax.ppermute(out, "row", perm)
                last_sent.append(got[k])
            for j, c in here.items():
                own[c][j] = out
                there[c][j] = got

    def lead(n):
        nonlocal token
        outs = call(
            functools.partial(lead_kernel, widths[:n]),
            [VMEM] * 8,
            [VMEM] * n,
            [f32(*packed(panel, w)) for w in widths[:n]],
            (*factors, rhs_own, rhs_sib),
            after=(token,),
        )
        token = outs[0]
        for c, out in enumerate(outs):
            got = {}
            for k in range(1, n_chip):
                got[k] = lax.ppermute(out, "row", [(i, PAIR * k + i) for i in range(PAIR)])
            own[c][0] = out
            there[c][0] = got

    find = functools.partial(block_at, n_leaf=n_leaf, targets_per=targets_per, nblocks=nblocks)

    def order(rows, own_list, flip):
        nonlocal token
        outs = call(
            functools.partial(order_kernel, find, n_leaf, flip),
            [SMEM] * 2 + [HBM],
            [VMEM] * 2,
            [bf16(n_leaf * BLK, piv)] * 2,
            (own_list, block_counts, rows),
            after=(token,),
            scratch=[pltpu.VMEM((4, BLK, piv), F32), pltpu.SemaphoreType.DMA((4,))],
        )
        token = outs[0]
        return outs

    def join(arrays, cuts):
        nonlocal token
        outs = call(
            functools.partial(join_kernel, cuts, len(arrays)),
            [VMEM] * len(arrays),
            [VMEM] * len(cuts),
            [f32(sum(p[2] for p in parts), TILE) for parts in cuts],
            arrays,
            after=(token,),
        )
        token = outs[0]
        return outs

    far = sorted(range(2, n_leaf, 2), key=lambda m: (m & -m) * 2 * n_leaf - m, reverse=True)
    held, flown = {}, {}
    updates = ()

    def unit(c):
        return packed(BLK, widths[c])[0] + (PAIR * TAIL if c == 0 else 0)

    def fly(c, sends):
        flown.setdefault(c, [])
        for m, a, qs in sends:
            got = lax.ppermute(a, "leaf", [(i, i ^ m) for i in range(n_leaf)])
            flown[c].append(got)
            held[c] += [(got, i * unit(c), q ^ m, first) for i, (q, first) in enumerate(qs)]

    def push(c, after=()):
        nonlocal token
        w = widths[c]
        n = unit(c)
        if c + 1 < n_chunk:
            groups = [(0, [0, 1])] + [(m, [m, m + 1]) for m in far]
        else:
            groups = [(m, [m]) for m in [0] + [m + i for m in far for i in range(PAIR)] + [1]]
        spots = {q: (k, i * n) for k, (_, qs) in enumerate(groups) for i, q in enumerate(qs)}
        places = [spots[q] for q in range(n_leaf)]
        tails = [(k, at + packed(BLK, w)[0]) for k, at in places] if c == 0 else None
        arrays, routes = [], {}
        for y in range(n_chip):
            for j in range(n_chip):
                a = own[c][j] if y == j else there[c][j][(y - j) % n_chip]
                k = next((k for k, b in enumerate(arrays) if b is a), len(arrays))
                if k == len(arrays):
                    arrays.append(a)
                routes[y, j] = k
        maps = (owners, owners_sib, block_counts) if c == 0 else ()
        outs = call(
            functools.partial(update_kernel, n_chip, places, w, routes, tails, find),
            [SMEM] * len(maps) + [VMEM] * (4 + len(arrays)),
            [VMEM] * len(groups),
            [f32(len(qs) * n, TILE) for _, qs in groups],
            (*maps, *updates, *arrays),
            after=(token, *after),
            scratch=[pltpu.VMEM((piv, 2 * w), BF16)],
        )
        token = outs[0]
        held[c] = [(outs[0], i * n, q, q) for i, q in enumerate(groups[0][1])]
        fly(c, [(m, a, [(q, q) for q in qs]) for (m, qs), a in zip(groups[1:], outs[1:])])

    def turn(c, after=()):
        nonlocal token
        n = unit(c)
        masks = [1]
        arrays, cuts, going = [], [], []
        for m in masks:
            parts, qs = [], []
            for a, at, q, first in held[c]:
                if q == m:
                    k = next((k for k, b in enumerate(arrays) if b is a), len(arrays))
                    if k == len(arrays):
                        arrays.append(a)
                    parts.append((k, at, n))
                    qs.append((q, first))
            cuts.append(parts)
            going.append(qs)
        held[c] = [b for b in held[c] if b[2] == 0]
        fly(c, list(zip(masks, join(arrays, cuts, after), going)))

    def join(arrays, cuts, after=()):
        nonlocal token
        outs = call(
            functools.partial(join_kernel, cuts, len(arrays)),
            [VMEM] * len(arrays),
            [VMEM] * len(cuts),
            [f32(sum(p[2] for p in parts), TILE) for parts in cuts],
            arrays,
            after=(token, *after),
        )
        token = outs[0]
        return outs

    slots = None
    mine_cols, theirs_cols, cuts = [], [], []
    carry = None

    def finish(c, after=()):
        nonlocal token, slots, carry
        w = widths[c]
        arrays, blocks = [], []
        for a, at, _, _ in sorted(held[c], key=lambda b: b[3]):
            k = next((k for k, b in enumerate(arrays) if b is a), len(arrays))
            if k == len(arrays):
                arrays.append(a)
            blocks.append((k, at))
        tail = packed(BLK, w)[0] if c == 0 else None
        lookup = () if c == 0 else tuple(slots)
        merge = carry is not None
        hold = w < TILE and not merge
        shape = f32(anc_rows, 2 * w if merge else w)
        outs = call(
            functools.partial(sum_kernel, blocks, tail, w, len(arrays), merge),
            [SMEM] * len(lookup) + [VMEM] * (len(arrays) + (2 if merge else 0)),
            [VMEM] * 2 + ([SMEM] if c == 0 else []),
            [shape] * 2 + ([jax.ShapeDtypeStruct((n_leaf * PAIR,), jnp.int32)] if c == 0 else []),
            (*lookup, *arrays, *(carry or ())),
            after=(token, *after),
            scratch=[pltpu.VMEM((PAIR, anc_rows, w), F32)],
        )
        token = outs[0]
        if c == 0:
            slots = outs[2:]
        if hold:
            carry = (outs[0], outs[1])
            return
        carry = None
        mine_cols.append(outs[0])
        theirs_cols.append(outs[1])
        cuts.append((offsets[c] + w - shape.shape[1], shape.shape[1]))

    left_own = lower[:, :before]
    left_sib = sibling(lax.optimization_barrier((left_own, token))[0])
    lead(2)
    update_sib = sibling(lax.optimization_barrier((update, token))[0])
    updates = tuple(order(update, owners, 0))
    left = call(
        left_kernel, [VMEM] * 2, [VMEM] * 2, [bf16(pair_rows, before)] * 2, (left_own, left_sib), after=(token,)
    )
    token = left[0]
    stages = range(1, n_chip)
    for j in stages:
        step([(j, (0, 1))] + ([(0, (2, 3)[: n_chunk - 2])] if j == 1 else []))
    updates += tuple(order(update_sib, owners_sib, 1))
    push(0)
    push(1)
    for c in range(2, n_chunk + 1):
        before_last = list(last_sent)
        for j in stages:
            if c < n_chunk:
                step([(j, (c,))] + ([(0, (c + 2,))] if j == 1 and c + 2 < n_chunk else []))
        if c > 2:
            push(c - 1)
        turn(c - 2)
        if c > 2:
            finish(c - 3)
    c = n_chunk - 1
    flat, chunks = [], []
    for i in range(n_chunk):
        chunks.append((offsets[i], widths[i], [len(flat) + j for j in range(n_chip)]))
        flat += own[i]
    panel_mine, panel_theirs = call(
        functools.partial(panels_kernel, chunks, n_chip, len(flat)),
        [VMEM] * len(flat),
        [VMEM] * 2,
        [f32(panel, half)] * 2,
        tuple(flat),
        after=(token,),
    )
    token = panel_mine
    early = len(cuts)
    (theirs_early,) = join(theirs_cols, [[(k, 0, anc_rows) for k in range(early)]])
    other_early = sibling(theirs_early)
    panel_other = sibling(panel_theirs)
    finish(c)
    finish(c - 1)
    pieces = call(
        functools.partial(ancestor_kernel, half, cuts[:early]),
        [VMEM] * (3 + early),
        [VMEM] * (2 * early),
        [f32(anc_rows, w) for _, w in cuts[:early] * 2],
        (anc_inv, anc_rhs, *mine_cols[:early], other_early),
        after=(token,),
    )
    token = pieces[0]
    late = [sibling(a) for a in theirs_cols[early:]]
    parent, solved = call(
        functools.partial(last_kernel, half, cuts, early),
        [VMEM] * (4 + 2 * len(cuts)),
        [HBM] * 2,
        [f32(anc_rows, columns), f32(panel, columns)],
        (anc_inv, anc_rhs, panel_mine, panel_other, *pieces, *mine_cols[early:], *late),
        after=(token,),
        scratch=[pltpu.VMEM((anc_rows, w), F32) for _, w in cuts[early:] * 2]
        + [pltpu.SemaphoreType.DMA((2 * len(cuts) + 2,))],
    )
    return (solved[None], parent[None])


def solution(mesh):
    in_specs = (
        P("leaf", "row", None),
        P("leaf", "row", None),
        P("leaf", "row", None),
        P("leaf", "row", None),
        P("leaf", "row"),
        P("leaf"),
        P("leaf", "row", None),
        P("leaf", "row", None),
    )
    out_specs = (P("leaf", "row", None), P("leaf", "row", None))
    return jax.shard_map(body, mesh=mesh, in_specs=in_specs, out_specs=out_specs, check_vma=False)
```

```python
import functools

import jax
import jax.numpy as jnp
from jax import lax
from jax.experimental import pallas as pl
from jax.experimental.pallas import tpu as pltpu
from jax.sharding import PartitionSpec as P

BLK = 128
PAIR = 2
TILE = 128
TAIL = 8
VMEM_LIMIT = 16 * 1024 * 1024
FIRST_LIMIT = 56 * 1024 * 1024
F32 = jnp.float32
BF16 = jnp.bfloat16
ANY = pl.BlockSpec(memory_space=pl.ANY)
HBM = pl.BlockSpec(memory_space=pltpu.HBM)
VMEM = pl.BlockSpec(memory_space=pltpu.VMEM)
SMEM = pl.BlockSpec(memory_space=pltpu.SMEM)


def widths_of(half):
    assert half % TILE == 0
    return [TILE // 2] * 2 + [TILE] * (half // TILE - 1)


def mxu(a, b):
    return jnp.dot(a, b, preferred_element_type=F32)


def split(x):
    high = x.astype(BF16)
    return high, (x - high.astype(F32)).astype(BF16)


def both_terms(x):
    return jnp.concatenate(split(x), axis=1)


def product(high, low, x):
    w = x.shape[1] // 2
    wide = mxu(high, x)
    return wide[:, :w] + (wide[:, w:] + mxu(low, x[:, :w]))


def times(a, b):
    return product(*split(a), both_terms(b))


def f32(*shape):
    return jax.ShapeDtypeStruct(shape, F32)


def bf16(*shape):
    return jax.ShapeDtypeStruct(shape, BF16)


def packed(rows, w):
    return (rows, TILE) if w < TILE else (PAIR * rows, w)


def put(ref, at, even, odd):
    rows, w = even.shape
    if w < TILE:
        ref[at : at + rows, :] = jnp.concatenate([even, odd], axis=1)
    else:
        ref[at : at + rows, :] = even
        ref[at + rows : at + PAIR * rows, :] = odd


def get(ref, at, rows, w):
    if w < TILE:
        both = ref[at : at + rows, :]
        return both[:, :w], both[:, w:]
    return ref[at : at + rows, :], ref[at + rows : at + PAIR * rows, :]


def call(kernel, in_specs, out_specs, out_shape, operands, after=(), scratch=(), aliases=None, limit=VMEM_LIMIT):
    n = len(operands)
    extra = len(after)

    def run(*refs):
        kernel(*refs[:n], *refs[n + extra :])

    return pl.pallas_call(
        run,
        in_specs=list(in_specs) + [ANY] * extra,
        out_specs=out_specs,
        out_shape=out_shape,
        scratch_shapes=scratch,
        input_output_aliases=aliases or {},
        compiler_params=pltpu.CompilerParams(vmem_limit_bytes=limit),
        cost_estimate=pl.CostEstimate(flops=int(10e9), bytes_accessed=1, transcendentals=0),
    )(*operands, *after)


def fetch(pairs, sems):
    copies = [pltpu.make_async_copy(a, b, sems.at[i]) for i, (a, b) in enumerate(pairs)]
    for copy in copies:
        copy.start()
    return copies


def factor_kernel(inv, inv_sib, col, col_sib, even_h, even_l, odd_h, odd_l, cross_h, cross_l):
    def fill(even, odd, cross):
        even_h[...], even_l[...] = split(even[...])
        odd_h[...], odd_l[...] = split(odd[...])
        cross_h[...], cross_l[...] = split(cross[...])

    @pl.when(lax.axis_index("row") % PAIR == 1)
    def _():
        fill(inv_sib, inv, col)

    @pl.when(lax.axis_index("row") % PAIR == 0)
    def _():
        fill(inv, inv_sib, col_sib)


def left_kernel(left, left_sib, high, low):
    panel = left.shape[0]

    def fill(even, odd):
        high[:panel, :], low[:panel, :] = split(even[...])
        high[panel:, :], low[panel:, :] = split(odd[...])

    @pl.when(lax.axis_index("row") % PAIR == 1)
    def _():
        fill(left_sib, left)

    @pl.when(lax.axis_index("row") % PAIR == 0)
    def _():
        fill(left, left_sib)


def cut_kernel(cuts, n, *refs):
    srcs, outs, sems = refs[:n], refs[n:-1], refs[-1]
    odd = lax.rem(lax.axis_index("row"), PAIR)
    pairs = []
    for (k, kind), out in zip(cuts, outs):
        w = out.shape[1]
        at = {"first": 0, "mine": odd * w, "other": (1 - odd) * w, "panel": (lax.axis_index("row") // PAIR) * PAIR * w}[kind]
        for r in range(0, out.shape[0], TILE):
            rows = pl.ds(r, TILE)
            pairs.append((srcs[k].at[rows, pl.ds(pl.multiple_of(at, TILE), w)], out.at[rows, :]))
    for copy in fetch(pairs, sems):
        copy.wait()


def block_at(place, row, n_leaf, targets_per, nblocks, leaf, owners, counts):
    dest = leaf ^ place
    source, has, slot = jnp.int32(0), jnp.int32(0), jnp.int32(-1)
    for b in range(nblocks):
        hit = (lax.div(owners[b], jnp.int32(targets_per)) == dest) & (row * nblocks + b < counts[0])
        source = jnp.where(hit, b, source)
        has = jnp.where(hit, 1, has)
        slot = jnp.where(hit, lax.rem(owners[b], jnp.int32(targets_per)), slot)
    return source, has, slot


def order_kernel(find, n_leaf, flip, owners, counts, rows, high, low, buf, sems):
    row = lax.axis_index("row") ^ flip
    found = [find(s, row, leaf=lax.axis_index("leaf"), owners=owners, counts=counts) for s in range(n_leaf)]

    def copy(s):
        at = pl.multiple_of(found[s][0] * BLK, BLK)
        return pltpu.make_async_copy(rows.at[pl.ds(at, BLK), :], buf.at[s % 4], sems.at[s % 4])

    ahead = min(3, n_leaf)
    for s in range(ahead):
        copy(s).start()
    for s in range(n_leaf):
        if s + ahead < n_leaf:
            copy(s + ahead).start()
        copy(s).wait()
        here = slice(s * BLK, (s + 1) * BLK)

        @pl.when(found[s][1] == 1)
        def _(here=here, s=s):
            high[here, :], low[here, :] = split(buf[s % 4])

        @pl.when(found[s][1] == 0)
        def _(here=here):
            high[here, :] = jnp.zeros((BLK, high.shape[1]), BF16)
            low[here, :] = jnp.zeros((BLK, high.shape[1]), BF16)


def lead_kernel(widths, *refs):
    (inv_e, inv_o, cross), refs = [refs[i : i + 2] for i in range(0, 6, 2)], refs[6:]
    rhs_own, rhs_sib, outs = refs[0], refs[1], refs[2:]
    w = sum(widths)
    odd = lax.axis_index("row") % PAIR == 1

    @pl.when(lax.axis_index("row") // PAIR == 0)
    def _():
        own, sib = rhs_own[:, :w], rhs_sib[:, :w]
        even, other = jnp.where(odd, sib, own), jnp.where(odd, own, sib)
        x_even = product(inv_e[0][...], inv_e[1][...], both_terms(even))
        other = other - product(cross[0][...], cross[1][...], both_terms(x_even))
        x_odd = product(inv_o[0][...], inv_o[1][...], both_terms(other))
        at = 0
        for part, out in zip(widths, outs):
            put(out, 0, x_even[:, at : at + part], x_odd[:, at : at + part])
            at += part


def step_kernel(tasks, n_out, *refs):
    (inv_e, inv_o, cross, left), refs = [refs[i : i + 2] for i in range(0, 8, 2)], refs[8:]
    rhs_own, rhs_sib, refs = refs[0], refs[1], refs[2:]
    outs = refs[-n_out:]
    odd = lax.axis_index("row") % PAIR == 1
    chip = lax.axis_index("row") // PAIR
    panel = rhs_own.shape[0]
    used = 0
    for stage, first, widths, which in tasks:
        known = refs[used : used + stage * len(widths)]
        used += stage * len(widths)

        @pl.when(chip == stage)
        def _(stage=stage, first=first, widths=widths, known=known, which=which):
            w = sum(widths)
            own, sib = rhs_own[:, first : first + w], rhs_sib[:, first : first + w]
            even, other = jnp.where(odd, sib, own), jnp.where(odd, own, sib)
            if stage:
                rows = []
                for i in range(stage):
                    got = [get(known[i * len(widths) + k], 0, panel, part) for k, part in enumerate(widths)]
                    rows += [jnp.concatenate([g[side] for g in got], axis=1) for side in range(PAIR)]
                x = jnp.concatenate(rows, axis=0)
                cols = slice(0, stage * PAIR * panel)
                gone = product(left[0][:, cols], left[1][:, cols], both_terms(x))
                even, other = even - gone[:panel], other - gone[panel:]
            x_even = product(inv_e[0][...], inv_e[1][...], both_terms(even))
            other = other - product(cross[0][...], cross[1][...], both_terms(x_even))
            x_odd = product(inv_o[0][...], inv_o[1][...], both_terms(other))
            at = 0
            for part, k in zip(widths, which):
                put(outs[k], 0, x_even[:, at : at + part], x_odd[:, at : at + part])
                at += part


def update_kernel(n_chip, places, w, routes, tails, find, *refs):
    if tails is not None:
        owners, owners_sib, counts, refs = refs[0], refs[1], refs[2], refs[3:]
    high, low, high_sib, low_sib = refs[:4]
    n_in = 1 + max(routes.values())
    srcs, outs, x = refs[4 : 4 + n_in], refs[4 + n_in : -1], refs[-1]
    odd = lax.axis_index("row") % PAIR == 1
    chip = lax.axis_index("row") // PAIR
    panel = x.shape[0] // (PAIR * n_chip)
    for (y, j), k in routes.items():

        @pl.when(chip == y)
        def _(j=j, src=srcs[k]):
            even, other = get(src, 0, panel, w)
            at = j * PAIR * panel
            x[at : at + panel, :] = both_terms(even)
            x[at + panel : at + PAIR * panel, :] = both_terms(other)

    n_place = len(places)
    for s in sorted(range(0, n_place, PAIR), key=lambda s: -places[s][0]):
        rows = slice(s * BLK, (s + PAIR) * BLK)
        own = product(high[rows, :], low[rows, :], x[...])
        sib = product(high_sib[rows, :], low_sib[rows, :], x[...])
        even, other = jnp.where(odd, sib, own), jnp.where(odd, own, sib)
        for i in range(PAIR):
            k, at = places[s + i]
            part = slice(i * BLK, (i + 1) * BLK)
            put(outs[k], at, even[part], other[part])
    if tails is not None:
        for s, (k, at) in enumerate(tails):
            for flip, own_list in ((0, owners), (1, owners_sib)):
                row = lax.axis_index("row") ^ flip
                _, _, slot = find(s, row, leaf=lax.axis_index("leaf"), owners=own_list, counts=counts)
                here = pl.multiple_of(at + lax.rem(row, PAIR) * TAIL, TAIL)
                outs[k][pl.ds(here, TAIL), :] = jnp.full((TAIL, TILE), slot.astype(F32))


def sum_kernel(blocks, tail, w, n_src, merge, *refs):
    if tail is None:
        slots, refs = refs[0], refs[1:]
    srcs, refs = refs[:n_src], refs[n_src:]
    if merge:
        old_mine, old_theirs, refs = refs[0], refs[1], refs[2:]
    if tail is None:
        mine, theirs, total = refs
    else:
        mine, theirs, slots, total = refs
        for s, (k, at) in enumerate(blocks):
            for i in range(PAIR):
                here = slice(at + tail + i * TAIL, at + tail + (i + 1) * TAIL)
                slots[PAIR * s + i] = jnp.max(srcs[k][here, :]).astype(jnp.int32)
    odd = lax.axis_index("row") % PAIR == 1
    total[...] = jnp.zeros_like(total)
    for s, (k, at) in enumerate(blocks):
        got = get(srcs[k], at, BLK, w)
        for i in range(PAIR):
            slot = slots[PAIR * s + i]

            @pl.when(slot >= 0)
            def _(slot=slot, i=i, got=got):
                place = pl.ds(pl.multiple_of(slot * BLK, BLK), BLK)
                total[i, place, :] += got[i]

    a = jnp.where(odd, total[1], total[0])
    b = jnp.where(odd, total[0], total[1])
    if merge:
        a = jnp.concatenate([old_mine[...], a], axis=1)
        b = jnp.concatenate([old_theirs[...], b], axis=1)
    mine[...] = a
    theirs[...] = b


def solve_blocks(inv, rhs, at, total, put_rows):
    w = total.shape[1]
    for t in range(total.shape[0] // BLK):
        rows = slice(t * BLK, (t + 1) * BLK)
        put_rows(rows, times(inv[rows, :], rhs[rows, pl.ds(at, w)] - total[rows, :]))


def ancestor_kernel(half, cuts, inv, rhs, *refs):
    n = len(cuts)
    mine, other, outs = refs[:n], refs[n], refs[n + 1 :]
    odd = lax.rem(lax.axis_index("row"), PAIR)
    rows_all = inv.shape[0]
    for k, (first, _) in enumerate(cuts):
        for side, total, out in (
            (odd, mine[k], outs[k]),
            (1 - odd, other.at[k * rows_all : (k + 1) * rows_all, :], outs[n + k]),
        ):

            def put_rows(rows, x, out=out):
                out[rows, :] = x

            solve_blocks(inv, rhs, pl.multiple_of(side * half + first, TILE), total, put_rows)


def last_kernel(half, cuts, n_early, inv, rhs, panel_mine, panel_other, *refs):
    n = len(cuts)
    pieces, totals, out, solved = refs[: 2 * n_early], refs[2 * n_early : 2 * n], refs[2 * n], refs[2 * n + 1]
    scratch, sems = refs[2 * n + 2 : -1], refs[-1]
    odd = lax.rem(lax.axis_index("row"), PAIR)
    copies = []

    def send(src, dst, mine, first, w):
        at = pl.multiple_of((odd if mine else 1 - odd) * half + first, TILE)
        copy = pltpu.make_async_copy(src, dst.at[:, pl.ds(at, w)], sems.at[len(copies)])
        copy.start()
        copies.append(copy)

    for i in range(2 * n_early):
        send(pieces[i], out, i < n_early, *cuts[i % n_early])
    send(panel_mine, solved, True, 0, half)
    send(panel_other, solved, False, 0, half)
    late = n - n_early
    for i in range(2 * late):
        first, w = cuts[n_early + i % late]
        at = pl.multiple_of((odd if i < late else 1 - odd) * half + first, TILE)

        def put_rows(rows, x, buf=scratch[i]):
            buf[rows, :] = x

        solve_blocks(inv, rhs, at, totals[i], put_rows)
        send(scratch[i], out, i < late, first, w)
    for copy in copies:
        copy.wait()


def panels_kernel(chunks, n_chip, n_src, *refs):
    srcs, mine, theirs = refs[:n_src], refs[-2], refs[-1]
    odd = lax.axis_index("row") % PAIR == 1
    chip = lax.axis_index("row") // PAIR
    panel = mine.shape[0]
    for first, w, ks in chunks:
        for j in range(n_chip):

            @pl.when(chip == j)
            def _(src=srcs[ks[j]], first=first, w=w):
                even, other = get(src, 0, panel, w)
                mine[:, first : first + w] = jnp.where(odd, other, even)
                theirs[:, first : first + w] = jnp.where(odd, even, other)


def join_kernel(cuts, n, *refs):
    srcs, outs = refs[:n], refs[n:]
    for out, parts in zip(outs, cuts):
        at = 0
        for k, first, count in parts:
            out[at : at + count, :] = srcs[k][first : first + count, :]
            at += count


def body(
    right_side,
    lower_rows,
    diag_inverse,
    update_rows,
    owner_map,
    block_counts,
    ancestor_rhs,
    ancestor_inverse,
):
    n_row = lax.axis_size("row")
    n_leaf = lax.axis_size("leaf")
    my_row = lax.axis_index("row")
    my_leaf = lax.axis_index("leaf")
    side = my_row % PAIR
    n_chip = n_row // PAIR
    chip = my_row // PAIR
    rhs = right_side[0]
    lower = lower_rows[0]
    inverse = diag_inverse[0]
    update = update_rows[0]
    owners = owner_map[0]
    panel, columns = rhs.shape
    pair_rows = PAIR * panel
    half = columns // PAIR
    piv = update.shape[1]
    nblocks = update.shape[0] // BLK
    anc_rhs = ancestor_rhs[0]
    anc_inv = ancestor_inverse[0]
    anc_rows = anc_rhs.shape[0]
    targets_per = anc_rows // BLK

    widths = widths_of(half)
    offsets = [sum(widths[:i]) for i in range(len(widths))]
    n_chunk = len(widths)

    swap = [(r, r ^ 1) for r in range(n_row)]

    def sibling(a):
        return lax.ppermute(a, "row", swap)

    def across(a, mask):
        return lax.ppermute(a, "leaf", [(i, i ^ mask) for i in range(n_leaf)])

    def cut(arrays, cuts, after=(), limit=VMEM_LIMIT):
        return call(
            functools.partial(cut_kernel, [c[:2] for c in cuts], len(arrays)),
            [HBM] * len(arrays),
            [VMEM] * len(cuts),
            [f32(arrays[k].shape[0], w) for k, _, w in cuts],
            tuple(arrays),
            after=after,
            scratch=[pltpu.SemaphoreType.DMA((sum(arrays[k].shape[0] // TILE for k, _, _ in cuts),))],
            limit=limit,
        )

    col, rhs_own, rhs_out, inv_own = cut(
        [lower, rhs, inverse],
        [(0, "panel", panel), (1, "mine", half), (1, "other", half), (2, "first", panel)],
        limit=FIRST_LIMIT,
    )
    inv_sib = sibling(inverse)
    col_sib = sibling(col)
    rhs_sib = sibling(rhs_out)
    owners_sib = sibling(owners)
    before = max((n_chip - 1) * pair_rows, panel)

    factors = call(
        factor_kernel,
        [VMEM] * 4,
        [VMEM] * 6,
        [bf16(panel, panel)] * 6,
        (inv_own, inv_sib, col, col_sib),
        after=(rhs_sib, owners_sib),
    )
    token = factors[0]
    left = None

    own = [[None] * n_chip for _ in range(n_chunk)]
    there = [[None] * n_chip for _ in range(n_chunk)]
    last_sent = []

    def step(tasks, after=()):
        nonlocal token, last_sent
        if not tasks:
            return
        kinds, places = [], []
        for j, cs in tasks:
            place = []
            for c in cs:
                k = next((k for k, (w, js) in enumerate(kinds) if w == widths[c] and j not in js), len(kinds))
                if k == len(kinds):
                    kinds.append((widths[c], {}))
                kinds[k][1][j] = c
                place.append(k)
            places.append(place)
        known = [there[c][i][(j - i) % n_chip] for j, cs in tasks for i in range(j) for c in cs]
        lefts = left if left is not None else factors[4:6]
        plan = [(j, offsets[cs[0]], [widths[c] for c in cs], place) for (j, cs), place in zip(tasks, places)]
        outs = call(
            functools.partial(step_kernel, plan, len(kinds)),
            [VMEM] * (10 + len(known)),
            [VMEM] * len(kinds),
            [f32(*packed(panel, w)) for w, _ in kinds],
            (*factors, *lefts, rhs_own, rhs_sib, *known),
            after=(token, *after),
        )
        token = outs[0]
        last_sent = []
        for (w, here), out in zip(kinds, outs):
            got = {}
            for k in range(1, n_chip):
                perm = []
                for j in here:
                    to = (j + k) % n_chip
                    perm += [(PAIR * j + i, PAIR * to + i) for i in range(PAIR)]
                got[k] = lax.ppermute(out, "row", perm)
                last_sent.append(got[k])
            for j, c in here.items():
                own[c][j] = out
                there[c][j] = got

    def lead(n):
        nonlocal token
        outs = call(
            functools.partial(lead_kernel, widths[:n]),
            [VMEM] * 8,
            [VMEM] * n,
            [f32(*packed(panel, w)) for w in widths[:n]],
            (*factors, rhs_own, rhs_sib),
            after=(token,),
        )
        token = outs[0]
        for c, out in enumerate(outs):
            got = {}
            for k in range(1, n_chip):
                got[k] = lax.ppermute(out, "row", [(i, PAIR * k + i) for i in range(PAIR)])
            own[c][0] = out
            there[c][0] = got

    find = functools.partial(block_at, n_leaf=n_leaf, targets_per=targets_per, nblocks=nblocks)

    def order(rows, own_list, flip):
        nonlocal token
        outs = call(
            functools.partial(order_kernel, find, n_leaf, flip),
            [SMEM] * 2 + [HBM],
            [VMEM] * 2,
            [bf16(n_leaf * BLK, piv)] * 2,
            (own_list, block_counts, rows),
            after=(token,),
            scratch=[pltpu.VMEM((4, BLK, piv), F32), pltpu.SemaphoreType.DMA((4,))],
        )
        token = outs[0]
        return outs

    def join(arrays, cuts):
        nonlocal token
        outs = call(
            functools.partial(join_kernel, cuts, len(arrays)),
            [VMEM] * len(arrays),
            [VMEM] * len(cuts),
            [f32(sum(p[2] for p in parts), TILE) for parts in cuts],
            arrays,
            after=(token,),
        )
        token = outs[0]
        return outs

    far = sorted(range(2, n_leaf, 2), key=lambda m: (m & -m) * 2 * n_leaf - m, reverse=True)
    held, flown = {}, {}
    updates = ()

    def unit(c):
        return packed(BLK, widths[c])[0] + (PAIR * TAIL if c == 0 else 0)

    def fly(c, sends):
        flown.setdefault(c, [])
        for m, a, qs in sends:
            got = lax.ppermute(a, "leaf", [(i, i ^ m) for i in range(n_leaf)])
            flown[c].append(got)
            held[c] += [(got, i * unit(c), q ^ m, first) for i, (q, first) in enumerate(qs)]

    def push(c, after=()):
        nonlocal token
        w = widths[c]
        n = unit(c)
        if c + 1 < n_chunk:
            groups = [(0, [0, 1])] + [(m, [m, m + 1]) for m in far]
        else:
            groups = [(m, [m]) for m in [0] + [m + i for m in far for i in range(PAIR)] + [1]]
        spots = {q: (k, i * n) for k, (_, qs) in enumerate(groups) for i, q in enumerate(qs)}
        places = [spots[q] for q in range(n_leaf)]
        tails = [(k, at + packed(BLK, w)[0]) for k, at in places] if c == 0 else None
        arrays, routes = [], {}
        for y in range(n_chip):
            for j in range(n_chip):
                a = own[c][j] if y == j else there[c][j][(y - j) % n_chip]
                k = next((k for k, b in enumerate(arrays) if b is a), len(arrays))
                if k == len(arrays):
                    arrays.append(a)
                routes[y, j] = k
        maps = (owners, owners_sib, block_counts) if c == 0 else ()
        outs = call(
            functools.partial(update_kernel, n_chip, places, w, routes, tails, find),
            [SMEM] * len(maps) + [VMEM] * (4 + len(arrays)),
            [VMEM] * len(groups),
            [f32(len(qs) * n, TILE) for _, qs in groups],
            (*maps, *updates, *arrays),
            after=(token, *after),
            scratch=[pltpu.VMEM((piv, 2 * w), BF16)],
        )
        token = outs[0]
        held[c] = [(outs[0], i * n, q, q) for i, q in enumerate(groups[0][1])]
        fly(c, [(m, a, [(q, q) for q in qs]) for (m, qs), a in zip(groups[1:], outs[1:])])

    def turn(c, after=()):
        nonlocal token
        n = unit(c)
        masks = [1]
        arrays, cuts, going = [], [], []
        for m in masks:
            parts, qs = [], []
            for a, at, q, first in held[c]:
                if q == m:
                    k = next((k for k, b in enumerate(arrays) if b is a), len(arrays))
                    if k == len(arrays):
                        arrays.append(a)
                    parts.append((k, at, n))
                    qs.append((q, first))
            cuts.append(parts)
            going.append(qs)
        held[c] = [b for b in held[c] if b[2] == 0]
        fly(c, list(zip(masks, join(arrays, cuts, after), going)))

    def join(arrays, cuts, after=()):
        nonlocal token
        outs = call(
            functools.partial(join_kernel, cuts, len(arrays)),
            [VMEM] * len(arrays),
            [VMEM] * len(cuts),
            [f32(sum(p[2] for p in parts), TILE) for parts in cuts],
            arrays,
            after=(token, *after),
        )
        token = outs[0]
        return outs

    slots = None
    mine_cols, theirs_cols, cuts = [], [], []
    carry = None

    def finish(c, after=()):
        nonlocal token, slots, carry
        w = widths[c]
        arrays, blocks = [], []
        for a, at, _, _ in sorted(held[c], key=lambda b: b[3]):
            k = next((k for k, b in enumerate(arrays) if b is a), len(arrays))
            if k == len(arrays):
                arrays.append(a)
            blocks.append((k, at))
        tail = packed(BLK, w)[0] if c == 0 else None
        lookup = () if c == 0 else tuple(slots)
        merge = carry is not None
        hold = w < TILE and not merge
        shape = f32(anc_rows, 2 * w if merge else w)
        outs = call(
            functools.partial(sum_kernel, blocks, tail, w, len(arrays), merge),
            [SMEM] * len(lookup) + [VMEM] * (len(arrays) + (2 if merge else 0)),
            [VMEM] * 2 + ([SMEM] if c == 0 else []),
            [shape] * 2 + ([jax.ShapeDtypeStruct((n_leaf * PAIR,), jnp.int32)] if c == 0 else []),
            (*lookup, *arrays, *(carry or ())),
            after=(token, *after),
            scratch=[pltpu.VMEM((PAIR, anc_rows, w), F32)],
        )
        token = outs[0]
        if c == 0:
            slots = outs[2:]
        if hold:
            carry = (outs[0], outs[1])
            return
        carry = None
        mine_cols.append(outs[0])
        theirs_cols.append(outs[1])
        cuts.append((offsets[c] + w - shape.shape[1], shape.shape[1]))

    left_own = lower[:, :before]
    left_sib = sibling(lax.optimization_barrier((left_own, token))[0])
    lead(2)
    update_sib = sibling(lax.optimization_barrier((update, token))[0])
    updates = tuple(order(update, owners, 0))
    left = call(
        left_kernel, [VMEM] * 2, [VMEM] * 2, [bf16(pair_rows, before)] * 2, (left_own, left_sib), after=(token,)
    )
    token = left[0]
    stages = range(1, n_chip)
    for j in stages:
        step([(j, (0, 1))] + ([(0, (2, 3)[: n_chunk - 2])] if j == 1 else []))
    updates += tuple(order(update_sib, owners_sib, 1))
    push(0)
    push(1)
    for c in range(2, n_chunk + 1):
        before_last = list(last_sent)
        for j in stages:
            if c < n_chunk:
                step([(j, (c,))] + ([(0, (c + 2,))] if j == 1 and c + 2 < n_chunk else []))
        if c > 2:
            push(c - 1)
        turn(c - 2)
        if c > 2:
            finish(c - 3)
    c = n_chunk - 1
    flat, chunks = [], []
    for i in range(n_chunk):
        chunks.append((offsets[i], widths[i], [len(flat) + j for j in range(n_chip)]))
        flat += own[i]
    panel_mine, panel_theirs = call(
        functools.partial(panels_kernel, chunks, n_chip, len(flat)),
        [VMEM] * len(flat),
        [VMEM] * 2,
        [f32(panel, half)] * 2,
        tuple(flat),
        after=(token,),
    )
    token = panel_mine
    early = len(cuts)
    (theirs_early,) = join(theirs_cols, [[(k, 0, anc_rows) for k in range(early)]])
    other_early = sibling(theirs_early)
    panel_other = sibling(panel_theirs)
    finish(c)
    finish(c - 1)
    pieces = call(
        functools.partial(ancestor_kernel, half, cuts[:early]),
        [VMEM] * (3 + early),
        [VMEM] * (2 * early),
        [f32(anc_rows, w) for _, w in cuts[:early] * 2],
        (anc_inv, anc_rhs, *mine_cols[:early], other_early),
        after=(token,),
    )
    token = pieces[0]
    late = [sibling(a) for a in theirs_cols[early:]]
    parent, solved = call(
        functools.partial(last_kernel, half, cuts, early),
        [VMEM] * (4 + 2 * len(cuts)),
        [HBM] * 2,
        [f32(anc_rows, columns), f32(panel, columns)],
        (anc_inv, anc_rhs, panel_mine, panel_other, *pieces, *mine_cols[early:], *late),
        after=(token,),
        scratch=[pltpu.VMEM((anc_rows, w), F32) for _, w in cuts[early:] * 2]
        + [pltpu.SemaphoreType.DMA((2 * len(cuts) + 2,))],
    )
    return (solved[None], parent[None])


def solution(mesh):
    in_specs = (
        P("leaf", "row", None),
        P("leaf", "row", None),
        P("leaf", "row", None),
        P("leaf", "row", None),
        P("leaf", "row"),
        P("leaf"),
        P("leaf", "row", None),
        P("leaf", "row", None),
    )
    out_specs = (P("leaf", "row", None), P("leaf", "row", None))
    return jax.shard_map(body, mesh=mesh, in_specs=in_specs, out_specs=out_specs, check_vma=False)
```
